256 devices in a mesh: seq: 32 (over z, x), row: 4 (over y), col: 2 (over core).
Axes of the slice: x: 4, y: 4, z: 8, core: 2. Of those that a mesh axis runs over, the one named last changes fastest.
Arguments:
- tokens: bfloat16 [16384, 4608], P(('seq', 'row'), 'col')
- norm_gain: float32 [4608], replicated, may hold values from 0.5 to 2
- w_query: bfloat16 [4608, 2048], P('row', 'col'), may hold values from -0.09375 to 0.09375
- w_keyval: bfloat16 [4608, 2, 1024], P('row', None, 'col'), may hold values from -0.09375 to 0.09375
- active: int32 [32], replicated, may hold values from 64 to 512, as said below
Outputs:
- attended: bfloat16 [16384, 2048], P(('seq', 'row'), 'col')
The draws below stay inside these ranges and needn't reach their ends.
Inputs may be any that keep to these rules, and one draw needn't show every extreme that they name: active tokens of each shard form a prefix of it; in every draw one shard is wholly active.
All inputs are finite; a program needn't handle non-finite values.
Results may differ from the reference program's by a relative error of at most 0.0084.
Values may be sent and summed in bfloat16 or wider, within the bound.
No kernel may reach another device: no remote copies, remote signals or barrier semaphores. Data moves between devices by JAX's collectives and lax.ppermute only.
A program may use at most 192 MiB of HBM per device.

```python
import math
import jax
import jax.numpy as jnp
from jax import lax

D = 4608
HEADS = 16
KV_HEADS = 8
HEAD = 128
WINDOW = 4096
TOK_DEV = 512
TOKENS = 16384
SEQ_LEN = 8192
SHARDS = 32


def draw_tokens(key, part):
    key = jax.random.fold_in(key, 11)
    key_base, key_rows, key_cols = jax.random.split(key, 3)
    row_scale = jnp.exp(jax.random.uniform(key_rows, (TOKENS, 1), jnp.float32, 0.0, math.log(10.0)))
    col_scale = jnp.exp(jax.random.uniform(key_cols, (1, D), jnp.float32, 0.0, math.log(10.0))) / 3.0
    base = jax.random.normal(key_base, (TOKENS, D), jnp.float32)
    return (base * row_scale * col_scale).astype(jnp.bfloat16)


def draw_active(key, part):
    key = jax.random.fold_in(key, 23)
    key_base, key_full = jax.random.split(key)
    base = jax.random.randint(key_base, (SHARDS,), TOK_DEV // 8, TOK_DEV // 2 + 1, jnp.int32)
    full_index = jax.random.randint(key_full, (), 0, SHARDS, jnp.int32)
    return jnp.where(jnp.arange(SHARDS, dtype=jnp.int32) == full_index, TOK_DEV, base).astype(jnp.int32)


def levels(stream_key, dims, pieces, low, top_value):
    def one(dim, shards_of):
        heights = jax.random.uniform(jax.random.fold_in(jax.random.fold_in(stream_key, 6), dim), (shards_of,), jnp.float32, low / len(pieces), top_value / len(pieces))
        return jnp.repeat(jnp.exp(heights), dims[dim] // shards_of).reshape((-1,) + (1,) * (len(dims) - dim - 1))

    loudness = one(*pieces[0])
    for cut in pieces[1:]:
        loudness = loudness * one(*cut)
    return loudness


def scatter_about(key, extent, spread, most, shards=(), held_as=jnp.bfloat16):
    entries = spread * jax.random.normal(key, extent, jnp.float32)
    if shards:
        entries = entries * levels(key, extent, shards, -0.22, 0.18)
    return jnp.clip(entries, -most, most).astype(held_as)


def setup_inputs(seed: int = 0) -> dict:
    splits = jax.random.split(jax.random.key(seed), 6)
    return {
        "tokens": draw_tokens(jax.random.fold_in(splits[5], 71), 0),
        "norm_gain": jnp.clip(jnp.exp(jax.random.uniform(splits[1], (D,), jnp.float32, math.log(0.5), math.log(2.0))), 0.5, 2.0),
        "w_query": scatter_about(splits[2], (D, HEADS * HEAD), D ** -0.5, 0.09375, ((0, 4), (1, 2))),
        "w_keyval": scatter_about(splits[3], (D, 2, KV_HEADS * HEAD), D ** -0.5, 0.09375, ((0, 4), (2, 2))),
        "active": draw_active(jax.random.fold_in(splits[5], 71), 0),
    }


SCALE = 1.0 / 12.0
SOFTCAP = 50.0
EPSILON = 1e-06

def rotate(vectors, positions):
    half_width = vectors.shape[-1] // 2
    freqs = 10000.0 ** (-2.0 * jnp.arange(half_width, dtype=jnp.float32) / vectors.shape[-1])
    angles = positions.astype(jnp.float32)[:, None] * freqs[None, :]
    cosine = jnp.cos(angles)[:, None, :]
    sine = jnp.sin(angles)[:, None, :]
    first = vectors[..., :half_width]
    second = vectors[..., half_width:]
    return jnp.concatenate([first * cosine - second * sine, second * cosine + first * sine], -1)

def reference(tokens, norm_gain, w_query, w_keyval, active):
    total = tokens.shape[0]
    positions = jnp.arange(total, dtype=jnp.int32)
    in_sequence = positions % SEQ_LEN
    floated = tokens.astype(jnp.float32)
    meansq = lax.optimization_barrier(jnp.mean(floated * floated, -1, keepdims=True))
    normed = (floated * lax.rsqrt(meansq + EPSILON) * norm_gain).astype(jnp.bfloat16)
    query_raw = jnp.dot(normed, w_query, preferred_element_type=jnp.float32).reshape(total, HEADS, HEAD)
    query = rotate(query_raw, in_sequence).astype(jnp.bfloat16)
    keyval_raw = jnp.dot(normed, w_keyval.reshape(D, 2 * KV_HEADS * HEAD), preferred_element_type=jnp.float32)
    keyval_raw = keyval_raw.reshape(total, 2, KV_HEADS, HEAD)
    keys_all = rotate(keyval_raw[:, 0], in_sequence).astype(jnp.bfloat16)
    values_all = keyval_raw[:, 1].astype(jnp.bfloat16)
    live = positions % TOK_DEV < active[positions // TOK_DEV]
    keys_pad = jnp.concatenate([jnp.zeros((WINDOW, KV_HEADS, HEAD), jnp.bfloat16), keys_all], 0)
    values_pad = jnp.concatenate([jnp.zeros((WINDOW, KV_HEADS, HEAD), jnp.bfloat16), values_all], 0)
    live_pad = jnp.concatenate([jnp.zeros((WINDOW,), bool), live], 0)
    span_len = WINDOW + TOK_DEV

    def one_shard(index):
        first_row = (index * TOK_DEV).astype(jnp.int32)
        query_block = lax.dynamic_slice_in_dim(query, first_row, TOK_DEV, 0).astype(jnp.float32)
        query_block = query_block.reshape(TOK_DEV, KV_HEADS, HEADS // KV_HEADS, HEAD)
        key_block = lax.dynamic_slice_in_dim(keys_pad, first_row, span_len, 0).astype(jnp.float32)
        value_block = lax.dynamic_slice_in_dim(values_pad, first_row, span_len, 0).astype(jnp.float32)
        key_live = lax.dynamic_slice_in_dim(live_pad, first_row, span_len, 0)
        query_pos = first_row + jnp.arange(TOK_DEV, dtype=jnp.int32)
        key_pos = first_row - WINDOW + jnp.arange(span_len, dtype=jnp.int32)
        same_seq = jnp.floor_divide(key_pos[None, :] + SEQ_LEN * 4096, SEQ_LEN) == jnp.floor_divide(query_pos[:, None] + SEQ_LEN * 4096, SEQ_LEN)
        mask = key_live[None, :] & same_seq & (key_pos[None, :] <= query_pos[:, None]) & (key_pos[None, :] > query_pos[:, None] - WINDOW)
        scores = jnp.einsum('tgjd,kgd->tgjk', query_block, key_block) * SCALE
        scores = SOFTCAP * jnp.tanh(scores / SOFTCAP)
        weights = jnp.where(mask[:, None, None, :], jnp.exp(scores), 0.0).astype(jnp.bfloat16)
        denom = lax.optimization_barrier(jnp.sum(weights.astype(jnp.float32), -1))
        numer = jnp.einsum('tgjk,kgd->tgjd', weights.astype(jnp.float32), value_block)
        query_live = lax.dynamic_slice_in_dim(live, first_row, TOK_DEV, 0)
        safe = jnp.where(query_live[:, None, None], denom, 1.0)
        result = numer / safe[..., None]
        result = jnp.where(query_live[:, None, None, None], result, 0.0)
        return result.reshape(TOK_DEV, HEADS * HEAD).astype(jnp.bfloat16)
    blocks = lax.map(one_shard, jnp.arange(SHARDS, dtype=jnp.int32))
    return blocks.reshape(total, HEADS * HEAD)
```

```python
import functools
import math

import jax
import jax.numpy as jnp
from jax import lax
from jax.experimental import pallas as pl
from jax.experimental.pallas import tpu as pltpu
from jax.sharding import Mesh, PartitionSpec as P

SCALE = 1.0 / 12.0
SOFTCAP = 50.0
EPSILON = 1e-06

HEAD = 128
SHARD = 512
SEQ_SHARDS = 16
PLANE = 4
ROWS = 4
BLOCK = SHARD // ROWS
HALF = BLOCK // 2
MODEL = 4608
SLAB = MODEL // ROWS
CHUNK = 256
DEN_ROWS = 16
PIECE = BLOCK + DEN_ROWS
SEQ = ("z", "xh", "xl")

TO_TANH = SCALE / SOFTCAP
TO_EXP2 = SOFTCAP * math.log2(math.e)

bf16 = jnp.bfloat16
f32 = jnp.float32
VMEM = pl.BlockSpec(memory_space=pltpu.VMEM)
SMEM = pl.BlockSpec(memory_space=pltpu.SMEM)


def local(body, operands, out_shapes, name, scratch=(), flops=0, limit=40 * 2**20):
    return pl.pallas_call(
        body,
        out_shape=out_shapes,
        in_specs=[SMEM] + [VMEM] * (len(operands) - 1),
        out_specs=jax.tree.map(lambda _: VMEM, out_shapes),
        scratch_shapes=list(scratch),
        compiler_params=pltpu.CompilerParams(vmem_limit_bytes=limit),
        cost_estimate=pl.CostEstimate(flops=flops, bytes_accessed=2**20, transcendentals=0),
        name=name,
    )(*operands)


def scalars(ids):
    return ids[0], ids[1], ids[2]


def live_of(ids, shard):
    return ids[3 + shard]


def norm_body(ids, tokens, received, gain, out):
    _, _, core = scalars(ids)
    kept = tokens[pl.ds(pl.multiple_of(core * HALF, HALF), HALF), :].astype(f32)
    other = received[...].astype(f32)
    total = jnp.sum(kept * kept, -1, keepdims=True) + jnp.sum(other * other, -1, keepdims=True)
    inverse = lax.rsqrt(total * (1.0 / MODEL) + EPSILON)
    for part in range(2):
        span = slice(part * SLAB, (part + 1) * SLAB)
        mine, theirs = 2 * core + part, 2 * (1 - core) + part
        out[mine] = (kept[:, span] * inverse * gain[mine]).astype(bf16)
        out[theirs] = (other[:, span] * inverse * gain[theirs]).astype(bf16)


def keyval_partial_body(ids, mine, theirs, weights, out, joined):
    _, _, core = scalars(ids)
    for block in range(ROWS):
        joined[block, core] = mine[block]
        joined[block, 1 - core] = theirs[block]
    slab = joined[...].reshape(SHARD, SLAB)
    for target in range(ROWS):
        for part in range(2):
            start = part * ROWS * HEAD + target * HEAD
            out[target, :, part * HEAD : (part + 1) * HEAD] = jnp.dot(
                slab, weights[:, start : start + HEAD], preferred_element_type=f32
            ).astype(bf16)


def query_partial_body(ids, joined, weights, out):
    slab = joined[...].reshape(SHARD, SLAB)
    for target in range(ROWS):
        out[target] = jnp.dot(
            slab,
            weights[:, target * 2 * HEAD : (target + 1) * 2 * HEAD],
            preferred_element_type=f32,
        ).astype(bf16)


def rotate_body(rotated, ids, parts, cosine, sine, out):
    for block in range(ROWS):
        rows = slice(block * BLOCK, (block + 1) * BLOCK)
        total = parts[0, rows].astype(f32)
        for source in range(1, ROWS):
            total = total + parts[source, rows].astype(f32)
        for half in range(2):
            span = slice(half * HEAD, (half + 1) * HEAD)
            value = total[:, span]
            if half < rotated:
                value = value * cosine[rows] + pltpu.roll(value, HEAD // 2, 1) * sine[rows]
            out[rows, span] = value.astype(bf16)


def key_shards(shard):
    plane, place = shard >> 2, shard & 3
    mirror = PLANE - 1 - place
    chosen = jnp.where(place < 2, plane - 2, plane)
    return (
        shard,
        shard - PLANE,
        (plane - 1) * PLANE + mirror,
        shard - 2 * PLANE,
        chosen * PLANE + mirror,
    )


def mask_values(ids, key_shard, keyval, masked):
    shard = ids[0]
    first = (shard >> 4) << 4
    count = jnp.where(key_shard >= first, live_of(ids, jnp.maximum(key_shard, 0)), 0)
    for start in range(0, SHARD, CHUNK):

        @pl.when(start < count)
        def _():
            alive = (
                lax.broadcasted_iota(jnp.int32, (CHUNK, HEAD), 0) + start < count
            )
            rows = slice(start, start + CHUNK)
            values = keyval[rows, HEAD:].astype(f32)
            masked[rows, :HEAD] = jnp.where(alive, values, 0.0).astype(bf16)
            masked[rows, HEAD:] = jnp.where(alive, 1.0, 0.0).astype(bf16)

    return count


def accumulate(query, query_shard, query_count, blocks, sums, fresh):
    for start in range(0, SHARD, CHUNK):
        tokens = slice(start, start + CHUNK)
        place = start // CHUNK

        @pl.when(start < query_count)
        def _(tokens=tokens, place=place):
            if fresh:
                for head in range(2):
                    sums[head, tokens] = jnp.zeros((CHUNK, 2 * HEAD), f32)
            for key_shard, count, keyval, masked in blocks:
                back = query_shard - key_shard
                chunks = (count + (CHUNK - 1)) // CHUNK
                low = jnp.where(back == 2 * PLANE, place, 0)
                high = jnp.where(back == 0, jnp.minimum(chunks, place + 1), chunks)
                high = jnp.where((back >= 0) & (back <= 2 * PLANE), high, 0)
                edge = (back == 0) | (back == 2 * PLANE)

                def step(chunk, carry, keyval=keyval, masked=masked, back=back, edge=edge):
                    rows = pl.ds(pl.multiple_of(chunk * CHUNK, CHUNK), CHUNK)

                    def work(with_mask):
                        keys = keyval[rows, :HEAD]
                        values = masked[rows, :]
                        if with_mask:
                            key_at = lax.broadcasted_iota(jnp.int32, (CHUNK, CHUNK), 1)
                            query_at = lax.broadcasted_iota(jnp.int32, (CHUNK, CHUNK), 0)
                            ahead = jnp.where(key_at <= query_at, 1, 0)
                            seen = ahead == jnp.where(back == 0, 1, 0)
                        for head in range(2):
                            scores = lax.dot_general(
                                query[tokens, head * HEAD : (head + 1) * HEAD],
                                keys,
                                (((1,), (1,)), ((), ())),
                                preferred_element_type=f32,
                            )
                            weights = jnp.exp2(jnp.tanh(scores * TO_TANH) * TO_EXP2)
                            if with_mask:
                                weights = jnp.where(seen, weights, 0.0)
                            sums[head, tokens] += jnp.dot(
                                weights.astype(bf16), values, preferred_element_type=f32
                            )

                    masked_step = edge & (chunk == place)

                    @pl.when(masked_step)
                    def _():
                        work(True)

                    @pl.when(jnp.logical_not(masked_step))
                    def _():
                        work(False)

                    return carry

                lax.fori_loop(low, high, step, 0)


def early_body(ids, query, own, back1, mirror1, back2, sums, *masked):
    shard, _, _ = scalars(ids)
    shards = key_shards(shard)
    held = (own, back1, mirror1, back2)
    blocks = [
        (shards[i], mask_values(ids, shards[i], held[i], masked[i]), held[i], masked[i])
        for i in range(len(held))
    ]
    accumulate(query, shard, live_of(ids, shard), blocks, sums, True)


def late_body(ids, query, pair, own, back1, mirror1, back2, chosen, before, out, sums, pair_sums, *masked):
    shard, _, _ = scalars(ids)
    side = shard & 1
    partner = shard + 1 - 2 * side
    shards = key_shards(shard)
    held = (own, back1, mirror1, back2, chosen)
    blocks = [
        (shards[i], mask_values(ids, shards[i], held[i], masked[i]), held[i], masked[i])
        for i in range(len(held))
    ]
    count, pair_count = live_of(ids, shard), live_of(ids, partner)
    for start in range(0, SHARD, CHUNK):

        @pl.when(start < count)
        def _(start=start):
            for head in range(2):
                sums[head, start : start + CHUNK] = before[head, start : start + CHUNK]

    accumulate(query, shard, count, blocks[4:], sums, False)
    accumulate(pair, partner, pair_count, blocks, pair_sums, True)
    for held_sums, live, owner in ((sums, count, side), (pair_sums, pair_count, 1 - side)):
        for block in range(ROWS):
            start = block * BLOCK

            @pl.when(start < live)
            def _(held_sums=held_sums, owner=owner, block=block, start=start):
                target = owner * ROWS + block
                for head in range(2):
                    span = slice(head * HEAD, (head + 1) * HEAD)
                    out[target, :BLOCK, span] = held_sums[head, start : start + BLOCK, :HEAD].astype(bf16)
                    turned = held_sums[head, start : start + BLOCK, HEAD:].T[:8]
                    coarse = turned.astype(bf16).astype(f32)
                    out[target, BLOCK:, span] = jnp.concatenate([coarse, turned - coarse], 0).astype(bf16)


def finish_body(ids, pieces, out):
    shard, row, _ = scalars(ids)
    alive = lax.broadcasted_iota(jnp.int32, (BLOCK, HEAD), 0) + row * BLOCK < live_of(ids, shard)
    for group in range(ROWS):
        for head in range(2):
            span = slice(head * HEAD, (head + 1) * HEAD)
            numer = pieces[group, :BLOCK, span].astype(f32) + pieces[ROWS + group, :BLOCK, span].astype(f32)
            both = pieces[group, BLOCK:, span].astype(f32) + pieces[ROWS + group, BLOCK:, span].astype(f32)
            flat = both[0:1] + both[8:9]
            denom = jnp.broadcast_to(flat, (BLOCK, HEAD)).T
            result = jnp.where(alive, numer / jnp.where(alive, denom, 1.0), 0.0)
            start = group * 2 * HEAD + head * HEAD
            out[:, start : start + HEAD] = result.astype(bf16)


def along_seq(value, target):
    pairs = []
    for shard in range(32):
        to = target(shard // PLANE, shard % PLANE)
        if to is not None:
            pairs.append((shard, to[0] * PLANE + to[1]))
    return lax.ppermute(value, SEQ, pairs)


def hop(value):
    planes = SEQ_SHARDS // PLANE
    return along_seq(value, lambda z, x: (z + 1, x) if z % planes != planes - 1 else None)


def mirrored(value):
    return along_seq(value, lambda z, x: (z, PLANE - 1 - x))


def paired(value):
    return along_seq(value, lambda z, x: (z, x ^ 1))


def swapped(value):
    return lax.ppermute(value, "col", [(0, 1), (1, 0)])


def on_device(tokens, norm_gain, w_query, w_keyval, active):
    core = lax.axis_index("col")
    row = lax.axis_index("row")
    shard = lax.axis_index(SEQ)
    ids = jnp.concatenate([jnp.stack([shard, row, core]).astype(jnp.int32), active])
    sds = jax.ShapeDtypeStruct

    outgoing = lax.dynamic_slice_in_dim(tokens, (1 - core) * HALF, HALF, 0)
    received = swapped(outgoing)
    gain = norm_gain.reshape(ROWS, 1, SLAB)
    normed = local(
        norm_body, (ids, tokens, received, gain), sds((ROWS, HALF, SLAB), bf16), "norm"
    )
    mine = lax.all_to_all(normed, "row", 0, 0)
    theirs = swapped(mine)

    half = HEAD // 2
    positions = (shard % SEQ_SHARDS) * SHARD + jnp.arange(SHARD, dtype=jnp.int32)
    freqs = 10000.0 ** (-2.0 * jnp.arange(half, dtype=f32) / HEAD)
    angles = positions.astype(f32)[:, None] * freqs[None, :]
    cosine, sine = jnp.cos(angles), jnp.sin(angles)
    cosine = jnp.concatenate([cosine, cosine], 1)
    sine = jnp.concatenate([-sine, sine], 1)

    flat = w_keyval.reshape(SLAB, 2 * ROWS * HEAD)
    part = sds((ROWS, SHARD, 2 * HEAD), bf16)
    joined_shape = sds((ROWS, 2, HALF, SLAB), bf16)
    flops = 2 * SHARD * SLAB * 8 * HEAD
    keyval_part, joined = local(
        keyval_partial_body, (ids, mine, theirs, flat), (part, joined_shape), "keyval_partial", flops=flops
    )
    keyval_parts = lax.all_to_all(keyval_part, "row", 0, 0)
    query_part = local(query_partial_body, (ids, joined, w_query), part, "query_partial", flops=flops)
    held = sds((SHARD, 2 * HEAD), bf16)
    own = local(
        functools.partial(rotate_body, 1), (ids, keyval_parts, cosine, sine), held, "keyval_rotate"
    )
    query_parts = lax.all_to_all(query_part, "row", 0, 0)

    back1 = hop(own)
    back2 = hop(back1)
    mirror1 = mirrored(back1)
    chosen = mirrored(jnp.where(lax.axis_index("xh") == 0, own, back2))

    query = local(
        functools.partial(rotate_body, 2), (ids, query_parts, cosine, sine), held, "query_rotate"
    )
    pair = paired(query)

    sums_shape = (2, SHARD, 2 * HEAD)
    masked = pltpu.VMEM((SHARD, 2 * HEAD), bf16)
    before = local(
        early_body,
        (ids, query, own, back1, mirror1, back2),
        sds(sums_shape, f32),
        "attend_early",
        scratch=[masked] * 4,
        flops=2**31,
    )
    pieces = local(
        late_body,
        (ids, query, pair, own, back1, mirror1, back2, chosen, before),
        sds((2 * ROWS, PIECE, 2 * HEAD), bf16),
        "attend_late",
        scratch=[pltpu.VMEM(sums_shape, f32), pltpu.VMEM(sums_shape, f32)] + [masked] * 5,
        flops=2**31,
    )
    returned = lax.all_to_all(pieces, ("xl", "row"), 0, 0)
    return local(finish_body, (ids, returned), sds((BLOCK, ROWS * 2 * HEAD), bf16), "finish")


def solution(mesh):
    fine = Mesh(mesh.devices.reshape(8, 2, 2, ROWS, 2), SEQ + ("row", "col"))
    tokens_spec = P(SEQ + ("row",), "col")
    placed = (tokens_spec, P(), P("row", "col"), P("row", None, "col"), P())
    return jax.shard_map(
        on_device, mesh=fine, in_specs=placed, out_specs=tokens_spec, check_vma=False
    )
```

```python
import functools
import math

import jax
import jax.numpy as jnp
from jax import lax
from jax.experimental import pallas as pl
from jax.experimental.pallas import tpu as pltpu
from jax.sharding import Mesh, PartitionSpec as P

SCALE = 1.0 / 12.0
SOFTCAP = 50.0
EPSILON = 1e-06

HEAD = 128
SHARD = 512
SEQ_SHARDS = 16
PLANE = 4
ROWS = 4
BLOCK = SHARD // ROWS
HALF = BLOCK // 2
MODEL = 4608
SLAB = MODEL // ROWS
CHUNK = 256
TILE = 128
LISTED = 4 * SHARD + 4 * TILE
DEN_ROWS = 16
PIECE = BLOCK + DEN_ROWS
SEQ = ("z", "xh", "xl")

TO_TANH = SCALE / SOFTCAP
TO_EXP2 = SOFTCAP * math.log2(math.e)

bf16 = jnp.bfloat16
f32 = jnp.float32
VMEM = pl.BlockSpec(memory_space=pltpu.VMEM)
SMEM = pl.BlockSpec(memory_space=pltpu.SMEM)
FAR = pl.BlockSpec(memory_space=pltpu.HBM)


def local(body, operands, out_shapes, name, scratch=(), flops=0, limit=8 * 2**20, apart=()):
    return pl.pallas_call(
        body,
        out_shape=out_shapes,
        in_specs=[SMEM] + [FAR if i in apart else VMEM for i in range(1, len(operands))],
        out_specs=jax.tree.map(lambda _: VMEM, out_shapes),
        scratch_shapes=list(scratch),
        compiler_params=pltpu.CompilerParams(vmem_limit_bytes=limit),
        cost_estimate=pl.CostEstimate(flops=flops, bytes_accessed=2**20, transcendentals=0),
        name=name,
    )(*operands)


def scalars(ids):
    return ids[0], ids[1], ids[2]


def live_of(ids, shard):
    return ids[3 + shard]


def norm_body(ids, tokens, received, gain, out, held, arrived):
    _, _, core = scalars(ids)
    half = pl.ds(pl.multiple_of(core * HALF, HALF), HALF)
    copy = pltpu.make_async_copy(tokens.at[half, :], held, arrived)
    copy.start()
    other = received[half, :].astype(f32)
    total = jnp.sum(other * other, -1, keepdims=True)
    copy.wait()
    kept = held[...].astype(f32)
    total = total + jnp.sum(kept * kept, -1, keepdims=True)
    inverse = lax.rsqrt(total * (1.0 / MODEL) + EPSILON)
    for part in range(2):
        span = slice(part * SLAB, (part + 1) * SLAB)
        for value, slab in ((kept, 2 * core + part), (other, 2 * (1 - core) + part)):
            scale = gain[:, pl.ds(pl.multiple_of(slab * SLAB, HEAD), SLAB)]
            out[slab] = (value[:, span] * inverse * scale).astype(bf16)


def partial_body(steps, split, ids, mine, theirs, weights, *outs):
    _, row, core = scalars(ids)
    for step, out in zip(steps, outs):
        target = (row + step) & (ROWS - 1)
        if split:
            columns = [
                weights[:, pl.ds(pl.multiple_of((part * ROWS + target) * HEAD, HEAD), HEAD)]
                for part in range(2)
            ]
            columns = jnp.concatenate(columns, 1)
        else:
            columns = weights[:, pl.ds(pl.multiple_of(target * 2 * HEAD, 2 * HEAD), 2 * HEAD)]
        for slab, side in ((mine, core), (theirs, 1 - core)):
            rows = slab[...].reshape(ROWS * HALF, SLAB)
            sums = jnp.dot(rows, columns, preferred_element_type=f32).astype(bf16)
            for block in range(ROWS):
                value = sums[block * HALF : (block + 1) * HALF]
                out[block, side] = value


def rotate_body(rotated, ids, *refs):
    parts, (cosine, sine, out) = refs[:-3], refs[-3:]
    if len(parts) == 1:
        parts = [parts[0].at[source] for source in range(ROWS)]
    for block in range(ROWS):
        rows = slice(block * BLOCK, (block + 1) * BLOCK)
        total = parts[0][rows].astype(f32)
        for part in parts[1:]:
            total = total + part[rows].astype(f32)
        for half in range(2):
            span = slice(half * HEAD, (half + 1) * HEAD)
            value = total[:, span]
            if half < rotated:
                value = value * cosine[rows] + pltpu.roll(value, HEAD // 2, 1) * sine[rows]
            out[rows, span] = value.astype(bf16)


def key_shards(shard):
    plane, place = shard >> 2, shard & 3
    mirror = PLANE - 1 - place
    chosen = jnp.where(place < 2, plane - 2, plane)
    return (
        shard,
        shard - PLANE,
        (plane - 1) * PLANE + mirror,
        shard - 2 * PLANE,
        chosen * PLANE + mirror,
    )


def mask_values(ids, key_shard, keyval, masked):
    shard = ids[0]
    first = (shard >> 4) << 4
    count = jnp.where(key_shard >= first, live_of(ids, jnp.maximum(key_shard, 0)), 0)
    for start in range(0, SHARD, CHUNK):

        @pl.when(start < count)
        def _():
            alive = (
                lax.broadcasted_iota(jnp.int32, (CHUNK, HEAD), 0) + start < count
            )
            rows = slice(start, start + CHUNK)
            values = keyval[rows, HEAD:].astype(f32)
            masked[rows, :HEAD] = jnp.where(alive, values, 0.0).astype(bf16)
            masked[rows, HEAD:] = jnp.where(alive, 1.0, 0.0).astype(bf16)

    return count


def accumulate(query, query_shard, query_count, blocks, sums, fresh):
    for start in range(0, SHARD, CHUNK):
        tokens = slice(start, start + CHUNK)
        place = start // CHUNK

        @pl.when(start < query_count)
        def _(tokens=tokens, place=place):
            if fresh:
                for head in range(2):
                    sums[head, tokens] = jnp.zeros((CHUNK, 2 * HEAD), f32)
            for key_shard, count, keyval, masked in blocks:
                back = query_shard - key_shard
                chunks = (count + (CHUNK - 1)) // CHUNK
                low = jnp.where(back == 2 * PLANE, place, 0)
                high = jnp.where(back == 0, jnp.minimum(chunks, place + 1), chunks)
                high = jnp.where((back >= 0) & (back <= 2 * PLANE), high, 0)
                edge = (back == 0) | (back == 2 * PLANE)

                def step(chunk, carry, keyval=keyval, masked=masked, back=back, edge=edge):
                    rows = pl.ds(pl.multiple_of(chunk * CHUNK, CHUNK), CHUNK)

                    def work(with_mask):
                        keys = keyval[rows, :HEAD]
                        values = masked[rows, :]
                        if with_mask:
                            key_at = lax.broadcasted_iota(jnp.int32, (CHUNK, CHUNK), 1)
                            query_at = lax.broadcasted_iota(jnp.int32, (CHUNK, CHUNK), 0)
                            ahead = jnp.where(key_at <= query_at, 1, 0)
                            seen = ahead == jnp.where(back == 0, 1, 0)
                        for head in range(2):
                            scores = lax.dot_general(
                                query[tokens, head * HEAD : (head + 1) * HEAD],
                                keys,
                                (((1,), (1,)), ((), ())),
                                preferred_element_type=f32,
                            )
                            weights = jnp.exp2(jnp.tanh(scores * TO_TANH) * TO_EXP2)
                            if with_mask:
                                weights = jnp.where(seen, weights, 0.0)
                            sums[head, tokens] += jnp.dot(
                                weights.astype(bf16), values, preferred_element_type=f32
                            )

                    masked_step = edge & (chunk == place)

                    @pl.when(masked_step)
                    def _():
                        work(True)

                    @pl.when(jnp.logical_not(masked_step))
                    def _():
                        work(False)

                    return carry

                lax.fori_loop(low, high, step, 0)


def early_body(ids, query, own, back1, mirror1, back2, sums, *masked):
    shard, _, _ = scalars(ids)
    shards = key_shards(shard)
    held = (own, back1, mirror1, back2)
    blocks = [
        (shards[i], mask_values(ids, shards[i], held[i], masked[i]), held[i], masked[i])
        for i in range(len(held))
    ]
    accumulate(query, shard, live_of(ids, shard), blocks, sums, True)


def late_body(
    ids, query, pair, own, back1, mirror1, back2, chosen, before, out, sums, pair_sums, keys, values
):
    shard, _, _ = scalars(ids)
    side = shard & 1
    partner = shard + 1 - 2 * side
    own_shard, back1_shard, mirror1_shard, back2_shard, chosen_shard = key_shards(shard)
    first = (shard >> 4) << 4
    used = 0
    listed = (
        (own, own_shard, side == 0),
        (back2, back2_shard, side == 1),
        (back1, back1_shard, True),
        (mirror1, mirror1_shard, True),
        (chosen, chosen_shard, True),
    )
    for keyval, key_shard, seen in listed:
        before_this = used
        counted = (key_shard >= first) & seen
        count = jnp.where(counted, live_of(ids, jnp.maximum(key_shard, 0)), 0)
        for start in range(0, SHARD, TILE):

            @pl.when(start < count)
            def _(keyval=keyval, start=start, used=used, count=count):
                alive = lax.broadcasted_iota(jnp.int32, (TILE, HEAD), 0) + start < count
                rows = pl.ds(pl.multiple_of(used * TILE + start, TILE), TILE)
                keys[rows, :] = keyval[start : start + TILE, :HEAD]
                value = keyval[start : start + TILE, HEAD:].astype(f32)
                values[rows, :HEAD] = jnp.where(alive, value, 0.0).astype(bf16)
                values[rows, HEAD:] = jnp.where(alive, 1.0, 0.0).astype(bf16)

        used = used + ((count + (TILE - 1)) >> 7)
    rows = pl.ds(pl.multiple_of(used * TILE, TILE), 3 * TILE)
    keys[rows, :] = jnp.zeros((3 * TILE, HEAD), bf16)
    values[rows, :] = jnp.zeros((3 * TILE, 2 * HEAD), bf16)

    def attend(query, live, low, width, sums):
        for start in range(0, SHARD, CHUNK):
            tokens = slice(start, start + CHUNK)

            @pl.when(start < live)
            def _(tokens=tokens):
                heads = [query[tokens, :HEAD], query[tokens, HEAD:]]
                stacked = jnp.concatenate(heads, 0)
                for head in range(2):
                    sums[head, tokens] = jnp.zeros((CHUNK, 2 * HEAD), f32)

                def step(index, carry):
                    at = pl.ds(pl.multiple_of((low + index * width) * TILE, TILE), width * TILE)
                    scores = lax.dot_general(
                        stacked, keys[at, :], (((1,), (1,)), ((), ())), preferred_element_type=f32
                    )
                    weights = jnp.exp2(jnp.tanh(scores * TO_TANH) * TO_EXP2).astype(bf16)
                    added = jnp.dot(weights, values[at, :], preferred_element_type=f32)
                    for head in range(2):
                        sums[head, tokens] += added[head * CHUNK : (head + 1) * CHUNK]
                    return carry

                lax.fori_loop(0, (used - low + (width - 1)) // width, step, 0)

    count, pair_count = live_of(ids, shard), live_of(ids, partner)
    attend(query, count, before_this, 2, sums)
    attend(pair, pair_count, 0, 4, pair_sums)
    same = lax.broadcasted_iota(jnp.int32, (BLOCK, HEAD), 0) == lax.broadcasted_iota(
        jnp.int32, (BLOCK, HEAD), 1
    )
    for held, live, owner, earlier in (
        (sums, count, side, before),
        (pair_sums, pair_count, 1 - side, None),
    ):
        for block in range(ROWS):
            start = block * BLOCK

            @pl.when(start < live)
            def _(held=held, owner=owner, earlier=earlier, block=block, start=start):
                target = owner * ROWS + block
                for head in range(2):
                    span = slice(head * HEAD, (head + 1) * HEAD)
                    total = held[head, start : start + BLOCK]
                    if earlier is not None:
                        total = total + earlier[head, start : start + BLOCK]
                    out[target, :BLOCK, span] = total[:, :HEAD].astype(bf16)
                    line = jnp.sum(jnp.where(same, total[:, HEAD:], 0.0), 0, keepdims=True)
                    line = jnp.broadcast_to(line, (8, HEAD))
                    coarse = line.astype(bf16).astype(f32)
                    out[target, BLOCK:, span] = jnp.concatenate([coarse, line - coarse], 0).astype(bf16)


def finish_body(ids, pieces, out):
    shard, row, _ = scalars(ids)
    at = lax.broadcasted_iota(jnp.int32, (BLOCK, HEAD), 0)
    same = at == lax.broadcasted_iota(jnp.int32, (BLOCK, HEAD), 1)
    alive = at + row * BLOCK < live_of(ids, shard)
    for group in range(ROWS):
        for head in range(2):
            span = slice(head * HEAD, (head + 1) * HEAD)
            numer = pieces[group, :BLOCK, span].astype(f32) + pieces[ROWS + group, :BLOCK, span].astype(f32)
            both = pieces[group, BLOCK:, span].astype(f32) + pieces[ROWS + group, BLOCK:, span].astype(f32)
            line = both[0:1] + both[8:9]
            denom = jnp.sum(jnp.where(same, line, 0.0), 1, keepdims=True)
            result = jnp.where(alive, numer * (1.0 / denom), 0.0)
            start = group * 2 * HEAD + head * HEAD
            out[:, start : start + HEAD] = result.astype(bf16)


def along_seq(value, target):
    pairs = []
    for shard in range(32):
        to = target(shard // PLANE, shard % PLANE)
        if to is not None:
            pairs.append((shard, to[0] * PLANE + to[1]))
    return lax.ppermute(value, SEQ, pairs)


def hop(value):
    planes = SEQ_SHARDS // PLANE
    return along_seq(value, lambda z, x: (z + 1, x) if z % planes != planes - 1 else None)


def mirrored(value):
    return along_seq(value, lambda z, x: (z, PLANE - 1 - x))


def paired(value):
    return along_seq(value, lambda z, x: (z, x ^ 1))


def onward(value, step):
    return lax.ppermute(value, "row", [(row, (row + step) % ROWS) for row in range(ROWS)])


def swapped(value):
    return lax.ppermute(value, "col", [(0, 1), (1, 0)])


def on_device(tokens, norm_gain, w_query, w_keyval, active):
    core = lax.axis_index("col")
    row = lax.axis_index("row")
    shard = lax.axis_index(SEQ)
    ids = jnp.concatenate([jnp.stack([shard, row, core]).astype(jnp.int32), active])
    sds = jax.ShapeDtypeStruct

    received = swapped(tokens)
    gain = norm_gain.reshape(1, MODEL)
    normed = local(
        norm_body,
        (ids, tokens, received, gain),
        sds((ROWS, HALF, SLAB), bf16),
        "norm",
        scratch=[pltpu.VMEM((HALF, ROWS * SLAB // 2), bf16), pltpu.SemaphoreType.DMA],
        apart=(1,),
    )
    mine = lax.all_to_all(normed, "row", 0, 0)
    mine, place = lax.optimization_barrier((mine, shard))
    theirs = swapped(mine)

    half = HEAD // 2
    positions = (place % SEQ_SHARDS) * SHARD + jnp.arange(SHARD, dtype=jnp.int32)
    freqs = 10000.0 ** (-2.0 * jnp.arange(half, dtype=f32) / HEAD)
    angles = positions.astype(f32)[:, None] * freqs[None, :]
    cosine, sine = jnp.cos(angles), jnp.sin(angles)
    cosine = jnp.concatenate([cosine, cosine], 1)
    sine = jnp.concatenate([-sine, sine], 1)

    flat = w_keyval.reshape(SLAB, 2 * ROWS * HEAD)
    held = sds((SHARD, 2 * HEAD), bf16)
    split = (ROWS, 2, HALF, 2 * HEAD)
    flops = 2 * SHARD * SLAB * 8 * HEAD

    def partial_sums(mine, theirs, weights, split_columns, steps, name):
        parts = local(
            functools.partial(partial_body, steps, split_columns),
            (ids, mine, theirs, weights),
            [sds(split, bf16)] * len(steps),
            name,
            flops=flops * len(steps) // ROWS,
        )
        return [value.reshape(SHARD, 2 * HEAD) for value in parts]

    (far,) = partial_sums(mine, theirs, flat, True, (2,), "keyval_far")
    mine, theirs, far = lax.optimization_barrier((mine, theirs, far))
    up, down, kept = partial_sums(mine, theirs, flat, True, (1, 3, 0), "keyval_near")
    mine, theirs, kept, cosine, sine = lax.optimization_barrier((mine, theirs, kept, cosine, sine))
    keyval_sums = (kept, onward(up, 1), onward(down, 3), onward(far, 2))
    steps = (2, 1, 3, 0)
    query_sums = partial_sums(mine, theirs, w_query, False, steps, "query_partial")
    own = local(
        functools.partial(rotate_body, 1), (ids, *keyval_sums, cosine, sine), held, "keyval_rotate"
    )
    query_sums, own = lax.optimization_barrier((query_sums, own))
    query_sums = [onward(value, step) if step else value for value, step in zip(query_sums, steps)]

    back1 = hop(own)
    back2 = hop(back1)
    mirror1 = mirrored(back1)
    chosen = mirrored(jnp.where(lax.axis_index("xh") == 0, own, back2))

    query_sums, back2_here = lax.optimization_barrier((query_sums, back2))
    query = local(
        functools.partial(rotate_body, 2), (ids, *query_sums, cosine, sine), held, "query_rotate"
    )
    pair = paired(query)

    sums_shape = (2, SHARD, 2 * HEAD)
    masked = pltpu.VMEM((SHARD, 2 * HEAD), bf16)
    before = local(
        early_body,
        (ids, query, own, back1, mirror1, back2_here),
        sds(sums_shape, f32),
        "attend_early",
        scratch=[masked] * 4,
        flops=2**31,
    )
    pieces = local(
        late_body,
        (ids, query, pair, own, back1, mirror1, back2_here, chosen, before),
        sds((2 * ROWS, PIECE, 2 * HEAD), bf16),
        "attend_late",
        scratch=[
            pltpu.VMEM(sums_shape, f32),
            pltpu.VMEM(sums_shape, f32),
            pltpu.VMEM((LISTED, HEAD), bf16),
            pltpu.VMEM((LISTED, 2 * HEAD), bf16),
        ],
        flops=2**31,
        limit=16 * 2**20,
    )
    returned = lax.all_to_all(pieces, ("xl", "row"), 0, 0)
    return local(finish_body, (ids, returned), sds((BLOCK, ROWS * 2 * HEAD), bf16), "finish")


def solution(mesh):
    fine = Mesh(mesh.devices.reshape(8, 2, 2, ROWS, 2), SEQ + ("row", "col"))
    tokens_spec = P(SEQ + ("row",), "col")
    placed = (tokens_spec, P(), P("row", "col"), P("row", None, "col"), P())
    return jax.shard_map(
        on_device, mesh=fine, in_specs=placed, out_specs=tokens_spec, check_vma=False
    )
```

```python
import functools
import math

import jax
import jax.numpy as jnp
from jax import lax
from jax.experimental import pallas as pl
from jax.experimental.pallas import tpu as pltpu
from jax.sharding import Mesh, PartitionSpec as P

SCALE = 1.0 / 12.0
SOFTCAP = 50.0
EPSILON = 1e-06

HEAD = 128
SHARD = 512
SEQ_SHARDS = 16
PLANE = 4
ROWS = 4
BLOCK = SHARD // ROWS
HALF = BLOCK // 2
MODEL = 4608
SLAB = MODEL // ROWS
CHUNK = 256
TILE = 128
LISTED = 4 * SHARD + 4 * TILE
DEN_ROWS = 16
PIECE = BLOCK + DEN_ROWS
SEQ = ("z", "xh", "xl")

TO_TANH = SCALE / SOFTCAP
TO_EXP2 = SOFTCAP * math.log2(math.e)

bf16 = jnp.bfloat16
f32 = jnp.float32
VMEM = pl.BlockSpec(memory_space=pltpu.VMEM)
SMEM = pl.BlockSpec(memory_space=pltpu.SMEM)
FAR = pl.BlockSpec(memory_space=pltpu.HBM)


def local(body, operands, out_shapes, name, scratch=(), flops=0, limit=8 * 2**20, specs=None):
    return pl.pallas_call(
        body,
        out_shape=out_shapes,
        in_specs=specs or [SMEM] + [VMEM] * (len(operands) - 1),
        out_specs=jax.tree.map(lambda _: VMEM, out_shapes),
        scratch_shapes=list(scratch),
        compiler_params=pltpu.CompilerParams(vmem_limit_bytes=limit),
        cost_estimate=pl.CostEstimate(flops=flops, bytes_accessed=2**20, transcendentals=0),
        name=name,
    )(*operands)


def scalars(ids):
    return ids[0], ids[1], ids[2]


def live_of(ids, shard):
    return ids[3 + shard]


def fetch_body(tokens, outgoing, kept, arrived):
    core = lax.axis_index("col")
    copies = []
    for index, (side, to) in enumerate(((1 - core, outgoing), (core, kept))):
        rows = pl.ds(pl.multiple_of(side * HALF, HALF), HALF)
        copies.append(pltpu.make_async_copy(tokens.at[rows, :], to, arrived.at[index]))
        copies[-1].start()
    for copy in copies:
        copy.wait()


def norm_body(ids, own, received, gain, out):
    _, _, core = scalars(ids)
    kept, other = own[...].astype(f32), received[...].astype(f32)
    total = jnp.sum(kept * kept, -1, keepdims=True) + jnp.sum(other * other, -1, keepdims=True)
    inverse = lax.rsqrt(total * (1.0 / MODEL) + EPSILON)
    for part in range(2):
        span = slice(part * SLAB, (part + 1) * SLAB)
        for value, slab in ((kept, 2 * core + part), (other, 2 * (1 - core) + part)):
            scale = gain[:, pl.ds(pl.multiple_of(slab * SLAB, HEAD), SLAB)]
            out[slab] = (value[:, span] * inverse * scale).astype(bf16)


def partial_body(steps, split, ids, mine, theirs, weights, *outs):
    _, row, core = scalars(ids)
    for step, out in zip(steps, outs):
        target = (row + step) & (ROWS - 1)
        if split:
            columns = [
                weights[:, pl.ds(pl.multiple_of((part * ROWS + target) * HEAD, HEAD), HEAD)]
                for part in range(2)
            ]
            columns = jnp.concatenate(columns, 1)
        else:
            columns = weights[:, pl.ds(pl.multiple_of(target * 2 * HEAD, 2 * HEAD), 2 * HEAD)]
        for slab, side in ((mine, core), (theirs, 1 - core)):
            rows = slab[...].reshape(ROWS * HALF, SLAB)
            sums = jnp.dot(rows, columns, preferred_element_type=f32)
            for block in range(ROWS):
                value = sums[block * HALF : (block + 1) * HALF]
                if len(outs) == 2:
                    outs[block // 2][block % 2, side] = value.astype(bf16)
                else:
                    out[block, side] = value.astype(out.dtype)


def join_body(ids, up, down, first, second, up_out, down_out):
    middle = SHARD // 2
    up_out[:middle] = (up[:middle] + first[...].astype(f32)).astype(bf16)
    up_out[middle:] = up[middle:].astype(bf16)
    down_out[:middle] = down[:middle].astype(bf16)
    down_out[middle:] = (down[middle:] + second[...].astype(f32)).astype(bf16)


def rotate_body(rotated, ids, *refs):
    parts, (cosine, sine, out) = refs[:-3], refs[-3:]
    if len(parts) == 1:
        parts = [parts[0].at[source] for source in range(ROWS)]
    for block in range(ROWS):
        rows = slice(block * BLOCK, (block + 1) * BLOCK)
        total = parts[0][rows].astype(f32)
        for part in parts[1:]:
            total = total + part[rows].astype(f32)
        for half in range(2):
            span = slice(half * HEAD, (half + 1) * HEAD)
            value = total[:, span]
            if half < rotated:
                value = value * cosine[rows] + pltpu.roll(value, HEAD // 2, 1) * sine[rows]
            out[rows, span] = value.astype(bf16)


def key_shards(shard):
    plane, place = shard >> 2, shard & 3
    mirror = PLANE - 1 - place
    chosen = jnp.where(place < 2, plane - 2, plane)
    return (
        shard,
        shard - PLANE,
        (plane - 1) * PLANE + mirror,
        shard - 2 * PLANE,
        chosen * PLANE + mirror,
    )


def mask_values(ids, key_shard, keyval, masked):
    shard = ids[0]
    first = (shard >> 4) << 4
    count = jnp.where(key_shard >= first, live_of(ids, jnp.maximum(key_shard, 0)), 0)
    for start in range(0, SHARD, CHUNK):

        @pl.when(start < count)
        def _():
            alive = (
                lax.broadcasted_iota(jnp.int32, (CHUNK, HEAD), 0) + start < count
            )
            rows = slice(start, start + CHUNK)
            values = keyval[rows, HEAD:].astype(f32)
            masked[rows, :HEAD] = jnp.where(alive, values, 0.0).astype(bf16)
            masked[rows, HEAD:] = jnp.where(alive, 1.0, 0.0).astype(bf16)

    return count


def accumulate(query, query_shard, query_count, blocks, sums, fresh):
    for start in range(0, SHARD, CHUNK):
        tokens = slice(start, start + CHUNK)
        place = start // CHUNK

        @pl.when(start < query_count)
        def _(tokens=tokens, place=place):
            if fresh:
                for head in range(2):
                    sums[head, tokens] = jnp.zeros((CHUNK, 2 * HEAD), f32)
            for key_shard, count, keyval, masked in blocks:
                back = query_shard - key_shard
                chunks = (count + (CHUNK - 1)) // CHUNK
                low = jnp.where(back == 2 * PLANE, place, 0)
                high = jnp.where(back == 0, jnp.minimum(chunks, place + 1), chunks)
                high = jnp.where((back >= 0) & (back <= 2 * PLANE), high, 0)
                edge = (back == 0) | (back == 2 * PLANE)

                def step(chunk, carry, keyval=keyval, masked=masked, back=back, edge=edge):
                    rows = pl.ds(pl.multiple_of(chunk * CHUNK, CHUNK), CHUNK)

                    def work(with_mask):
                        keys = keyval[rows, :HEAD]
                        values = masked[rows, :]
                        if with_mask:
                            key_at = lax.broadcasted_iota(jnp.int32, (CHUNK, CHUNK), 1)
                            query_at = lax.broadcasted_iota(jnp.int32, (CHUNK, CHUNK), 0)
                            ahead = jnp.where(key_at <= query_at, 1, 0)
                            seen = ahead == jnp.where(back == 0, 1, 0)
                        for head in range(2):
                            scores = lax.dot_general(
                                query[tokens, head * HEAD : (head + 1) * HEAD],
                                keys,
                                (((1,), (1,)), ((), ())),
                                preferred_element_type=f32,
                            )
                            weights = jnp.exp2(jnp.tanh(scores * TO_TANH) * TO_EXP2)
                            if with_mask:
                                weights = jnp.where(seen, weights, 0.0)
                            sums[head, tokens] += jnp.dot(
                                weights.astype(bf16), values, preferred_element_type=f32
                            )

                    masked_step = edge & (chunk == place)

                    @pl.when(masked_step)
                    def _():
                        work(True)

                    @pl.when(jnp.logical_not(masked_step))
                    def _():
                        work(False)

                    return carry

                lax.fori_loop(low, high, step, 0)


def early_body(ids, query, own, back1, mirror1, back2, sums, *masked):
    shard, _, _ = scalars(ids)
    shards = key_shards(shard)
    held = (own, back1, mirror1, back2)
    blocks = [
        (shards[i], mask_values(ids, shards[i], held[i], masked[i]), held[i], masked[i])
        for i in range(len(held))
    ]
    accumulate(query, shard, live_of(ids, shard), blocks, sums, True)


def late_body(
    ids, query, pair, own, back1, mirror1, back2, chosen, before, out, sums, pair_sums, keys, values
):
    shard, _, _ = scalars(ids)
    side = shard & 1
    partner = shard + 1 - 2 * side
    own_shard, back1_shard, mirror1_shard, back2_shard, chosen_shard = key_shards(shard)
    first = (shard >> 4) << 4
    used = 0
    listed = (
        (own, own_shard, side == 0),
        (back2, back2_shard, side == 1),
        (back1, back1_shard, True),
        (mirror1, mirror1_shard, True),
        (chosen, chosen_shard, True),
    )
    for place, (keyval, key_shard, seen) in enumerate(listed):
        if place == 4:
            common = used
        counted = (key_shard >= first) & seen
        count = jnp.where(counted, live_of(ids, jnp.maximum(key_shard, 0)), 0)
        for start in range(0, SHARD, TILE):

            @pl.when(start < count)
            def _(keyval=keyval, start=start, used=used, count=count):
                alive = lax.broadcasted_iota(jnp.int32, (TILE, HEAD), 0) + start < count
                rows = pl.ds(pl.multiple_of(used * TILE + start, TILE), TILE)
                keys[rows, :] = keyval[start : start + TILE, :HEAD]
                value = keyval[start : start + TILE, HEAD:].astype(f32)
                values[rows, :HEAD] = jnp.where(alive, value, 0.0).astype(bf16)
                values[rows, HEAD:] = jnp.where(alive, 1.0, 0.0).astype(bf16)

        used = used + ((count + (TILE - 1)) >> 7)
    rows = pl.ds(pl.multiple_of(used * TILE, TILE), 3 * TILE)
    keys[rows, :] = jnp.zeros((3 * TILE, HEAD), bf16)
    values[rows, :] = jnp.zeros((3 * TILE, 2 * HEAD), bf16)

    def attend(query, live, low, width, sums):
        for start in range(0, SHARD, CHUNK):
            tokens = slice(start, start + CHUNK)

            @pl.when(start < live)
            def _(tokens=tokens):
                heads = [query[tokens, :HEAD], query[tokens, HEAD:]]
                stacked = jnp.concatenate(heads, 0)
                for head in range(2):
                    sums[head, tokens] = jnp.zeros((CHUNK, 2 * HEAD), f32)

                def step(index, carry):
                    at = pl.ds(pl.multiple_of((low + index * width) * TILE, TILE), width * TILE)
                    scores = lax.dot_general(
                        stacked, keys[at, :], (((1,), (1,)), ((), ())), preferred_element_type=f32
                    )
                    weights = jnp.exp2(jnp.tanh(scores * TO_TANH) * TO_EXP2).astype(bf16)
                    added = jnp.dot(weights, values[at, :], preferred_element_type=f32)
                    for head in range(2):
                        sums[head, tokens] += added[head * CHUNK : (head + 1) * CHUNK]
                    return carry

                lax.fori_loop(0, (used - low + (width - 1)) // width, step, 0)

    count, pair_count = live_of(ids, shard), live_of(ids, partner)
    attend(query, count, common, 2, sums)
    attend(pair, pair_count, 0, 4, pair_sums)
    same = lax.broadcasted_iota(jnp.int32, (BLOCK, HEAD), 0) == lax.broadcasted_iota(
        jnp.int32, (BLOCK, HEAD), 1
    )
    for held, live, owner, earlier in (
        (sums, count, side, before),
        (pair_sums, pair_count, 1 - side, None),
    ):
        for block in range(ROWS):
            start = block * BLOCK

            @pl.when(start < live)
            def _(held=held, owner=owner, earlier=earlier, block=block, start=start):
                target = owner * ROWS + block
                for head in range(2):
                    span = slice(head * HEAD, (head + 1) * HEAD)
                    total = held[head, start : start + BLOCK]
                    if earlier is not None:
                        total = total + earlier[head, start : start + BLOCK]
                    out[target, :BLOCK, span] = total[:, :HEAD].astype(bf16)
                    line = jnp.sum(jnp.where(same, total[:, HEAD:], 0.0), 0, keepdims=True)
                    line = jnp.broadcast_to(line, (8, HEAD))
                    coarse = line.astype(bf16).astype(f32)
                    out[target, BLOCK:, span] = jnp.concatenate([coarse, line - coarse], 0).astype(bf16)


def finish_body(ids, pieces, out):
    shard, row, _ = scalars(ids)
    at = lax.broadcasted_iota(jnp.int32, (BLOCK, HEAD), 0)
    same = at == lax.broadcasted_iota(jnp.int32, (BLOCK, HEAD), 1)
    alive = at + row * BLOCK < live_of(ids, shard)
    for group in range(ROWS):
        for head in range(2):
            span = slice(head * HEAD, (head + 1) * HEAD)
            numer = pieces[group, :BLOCK, span].astype(f32) + pieces[ROWS + group, :BLOCK, span].astype(f32)
            both = pieces[group, BLOCK:, span].astype(f32) + pieces[ROWS + group, BLOCK:, span].astype(f32)
            line = both[0:1] + both[8:9]
            denom = jnp.sum(jnp.where(same, line, 0.0), 1, keepdims=True)
            result = jnp.where(alive, numer * (1.0 / denom), 0.0)
            start = group * 2 * HEAD + head * HEAD
            out[:, start : start + HEAD] = result.astype(bf16)


def along_seq(value, target):
    pairs = []
    for shard in range(32):
        to = target(shard // PLANE, shard % PLANE)
        if to is not None:
            pairs.append((shard, to[0] * PLANE + to[1]))
    return lax.ppermute(value, SEQ, pairs)


def hop(value):
    planes = SEQ_SHARDS // PLANE
    return along_seq(value, lambda z, x: (z + 1, x) if z % planes != planes - 1 else None)


def mirrored(value):
    return along_seq(value, lambda z, x: (z, PLANE - 1 - x))


def turned(value):
    planes = SEQ_SHARDS // PLANE

    def target(z, x):
        if x < PLANE // 2:
            return z, PLANE - 1 - x
        return (z + 1, PLANE - 1 - x) if z % planes != planes - 1 else None

    return along_seq(value, target)


def paired(value):
    return along_seq(value, lambda z, x: (z, x ^ 1))


def onward(value, step):
    return lax.ppermute(value, "row", [(row, (row + step) % ROWS) for row in range(ROWS)])


def swapped(value):
    return lax.ppermute(value, "col", [(0, 1), (1, 0)])


def on_device(tokens, norm_gain, w_query, w_keyval, active):
    core = lax.axis_index("col")
    row = lax.axis_index("row")
    shard = lax.axis_index(SEQ)
    ids = jnp.concatenate([jnp.stack([shard, row, core]).astype(jnp.int32), active])
    sds = jax.ShapeDtypeStruct

    half_shape = sds((HALF, MODEL // 2), bf16)
    outgoing, kept = local(
        fetch_body,
        (tokens,),
        (half_shape, half_shape),
        "fetch",
        scratch=[pltpu.SemaphoreType.DMA((2,))],
        specs=[FAR],
    )
    received = swapped(outgoing)
    gain = norm_gain.reshape(1, MODEL)
    normed = local(norm_body, (ids, kept, received, gain), sds((ROWS, HALF, SLAB), bf16), "norm")
    mine = lax.all_to_all(normed, "row", 0, 0)
    mine, place = lax.optimization_barrier((mine, shard))
    theirs = swapped(mine)

    half = HEAD // 2
    positions = (place % SEQ_SHARDS) * SHARD + jnp.arange(SHARD, dtype=jnp.int32)
    freqs = 10000.0 ** (-2.0 * jnp.arange(half, dtype=f32) / HEAD)
    angles = positions.astype(f32)[:, None] * freqs[None, :]
    cosine, sine = jnp.cos(angles), jnp.sin(angles)
    cosine = jnp.concatenate([cosine, cosine], 1)
    sine = jnp.concatenate([-sine, sine], 1)

    flat = w_keyval.reshape(SLAB, 2 * ROWS * HEAD)
    held = sds((SHARD, 2 * HEAD), bf16)
    split = (ROWS, 2, HALF, 2 * HEAD)
    flops = 2 * SHARD * SLAB * 8 * HEAD

    def sums_across(mine, theirs, weights, split_columns, steps, kind, name, count=1):
        parts = local(
            functools.partial(partial_body, steps, split_columns),
            (ids, mine, theirs, weights),
            [sds((ROWS // count,) + split[1:], kind)] * (len(steps) * count),
            name,
            flops=flops * len(steps) // ROWS,
        )
        return [value.reshape(SHARD // count, 2 * HEAD) for value in parts]

    def joined(up, down, first, second, name):
        return local(join_body, (ids, up, down, first, second), [held, held], name)

    first, second = sums_across(mine, theirs, flat, True, (2,), bf16, "keyval_far", 2)
    mine, theirs, first, second = lax.optimization_barrier((mine, theirs, first, second))
    first, second = onward(first, 1), onward(second, 3)
    up, down, kept = sums_across(mine, theirs, flat, True, (1, 3, 0), f32, "keyval_near")
    mine, theirs, kept, cosine, sine = lax.optimization_barrier((mine, theirs, kept, cosine, sine))
    up, down = joined(up, down, first, second, "keyval_join")
    mine, theirs, up, down = lax.optimization_barrier((mine, theirs, up, down))
    up, down = onward(up, 1), onward(down, 3)
    steps = (2, 1, 3, 0)
    query_sums = sums_across(mine, theirs, w_query, False, steps, bf16, "query_partial")
    own = local(
        functools.partial(rotate_body, 1), (ids, kept, up, down, cosine, sine), held, "keyval_rotate"
    )
    query_sums, own = lax.optimization_barrier((query_sums, own))
    query_sums = [onward(value, step) if step else value for value, step in zip(query_sums, steps)]

    back1 = hop(own)
    back2 = hop(back1)
    mirror1 = mirrored(back1)
    chosen = turned(jnp.where(lax.axis_index("xh") == 0, own, back1))

    query_sums, back2 = lax.optimization_barrier((query_sums, back2))
    query = local(
        functools.partial(rotate_body, 2), (ids, *query_sums, cosine, sine), held, "query_rotate"
    )
    pair = paired(query)

    sums_shape = (2, SHARD, 2 * HEAD)
    masked = pltpu.VMEM((SHARD, 2 * HEAD), bf16)
    before = local(
        early_body,
        (ids, query, own, back1, mirror1, back2),
        sds(sums_shape, f32),
        "attend_early",
        scratch=[masked] * 4,
        flops=2**31,
    )
    pieces = local(
        late_body,
        (ids, query, pair, own, back1, mirror1, back2, chosen, before),
        sds((2 * ROWS, PIECE, 2 * HEAD), bf16),
        "attend_late",
        scratch=[
            pltpu.VMEM(sums_shape, f32),
            pltpu.VMEM(sums_shape, f32),
            pltpu.VMEM((LISTED, HEAD), bf16),
            pltpu.VMEM((LISTED, 2 * HEAD), bf16),
        ],
        flops=2**31,
        limit=16 * 2**20,
    )
    returned = lax.all_to_all(pieces, ("xl", "row"), 0, 0)
    return local(finish_body, (ids, returned), sds((BLOCK, ROWS * 2 * HEAD), bf16), "finish")


def solution(mesh):
    fine = Mesh(mesh.devices.reshape(8, 2, 2, ROWS, 2), SEQ + ("row", "col"))
    tokens_spec = P(SEQ + ("row",), "col")
    placed = (tokens_spec, P(), P("row", "col"), P("row", None, "col"), P())
    return jax.shard_map(
        on_device, mesh=fine, in_specs=placed, out_specs=tokens_spec, check_vma=False
    )
```

```python
import functools
import math

import jax
import jax.numpy as jnp
from jax import lax
from jax.experimental import pallas as pl
from jax.experimental.pallas import tpu as pltpu
from jax.sharding import Mesh, PartitionSpec as P

SCALE = 1.0 / 12.0
SOFTCAP = 50.0
EPSILON = 1e-06

HEAD = 128
SHARD = 512
SEQ_SHARDS = 16
PLANE = 4
ROWS = 4
BLOCK = SHARD // ROWS
HALF = BLOCK // 2
MODEL = 4608
SLAB = MODEL // ROWS
CHUNK = 256
TILE = 128
LISTED = 4 * SHARD + 4 * TILE
DEN_ROWS = 16
PIECE = BLOCK + DEN_ROWS
SEQ = ("z", "xh", "xl")

TO_TANH = SCALE / SOFTCAP
TO_EXP2 = SOFTCAP * math.log2(math.e)

bf16 = jnp.bfloat16
f32 = jnp.float32
VMEM = pl.BlockSpec(memory_space=pltpu.VMEM)
SMEM = pl.BlockSpec(memory_space=pltpu.SMEM)
FAR = pl.BlockSpec(memory_space=pltpu.HBM)


def local(body, operands, out_shapes, name, scratch=(), flops=0, limit=8 * 2**20, specs=None):
    return pl.pallas_call(
        body,
        out_shape=out_shapes,
        in_specs=specs or [SMEM] + [VMEM] * (len(operands) - 1),
        out_specs=jax.tree.map(lambda _: VMEM, out_shapes),
        scratch_shapes=list(scratch),
        compiler_params=pltpu.CompilerParams(vmem_limit_bytes=limit),
        cost_estimate=pl.CostEstimate(flops=flops, bytes_accessed=2**20, transcendentals=0),
        name=name,
    )(*operands)


def scalars(ids):
    return ids[0], ids[1], ids[2]


def live_of(ids, shard):
    return ids[3 + shard]


def fetch_body(tokens, outgoing, kept, arrived):
    core = lax.axis_index("col")
    copies = []
    for index, (side, to) in enumerate(((1 - core, outgoing), (core, kept))):
        rows = pl.ds(pl.multiple_of(side * HALF, HALF), HALF)
        copies.append(pltpu.make_async_copy(tokens.at[rows, :], to, arrived.at[index]))
        copies[-1].start()
    for copy in copies:
        copy.wait()


def norm_body(ids, own, received, gain, *refs):
    outs, whole = refs[:ROWS], refs[ROWS]
    _, row, core = scalars(ids)
    kept, other = own[...].astype(f32), received[...].astype(f32)
    total = jnp.sum(kept * kept, -1, keepdims=True) + jnp.sum(other * other, -1, keepdims=True)
    inverse = lax.rsqrt(total * (1.0 / MODEL) + EPSILON)
    for part in range(2):
        span = slice(part * SLAB, (part + 1) * SLAB)
        for value, slab in ((kept, 2 * core + part), (other, 2 * (1 - core) + part)):
            scale = gain[:, pl.ds(pl.multiple_of(slab * SLAB, HEAD), SLAB)]
            whole[slab] = (value[:, span] * inverse * scale).astype(bf16)
    for step in range(ROWS):
        outs[step][...] = whole[(row + step) & (ROWS - 1)]


def partial_body(steps, split, ids, *refs):
    mine, theirs, weights, outs = refs[:ROWS], refs[ROWS : 2 * ROWS], refs[2 * ROWS], refs[2 * ROWS + 1 :]
    _, row, core = scalars(ids)
    for step, out in zip(steps, outs):
        target = (row + step) & (ROWS - 1)
        if split:
            columns = [
                weights[:, pl.ds(pl.multiple_of((part * ROWS + target) * HEAD, HEAD), HEAD)]
                for part in range(2)
            ]
            columns = jnp.concatenate(columns, 1)
        else:
            columns = weights[:, pl.ds(pl.multiple_of(target * 2 * HEAD, 2 * HEAD), 2 * HEAD)]
        for pieces, side in ((mine, core), (theirs, 1 - core)):
            rows = jnp.concatenate([piece[...] for piece in pieces], 0)
            sums = jnp.dot(rows, columns, preferred_element_type=f32).astype(out.dtype)
            for back in range(ROWS):
                block = (row - back) & (ROWS - 1)
                value = sums[back * HALF : (back + 1) * HALF]
                if len(outs) == len(steps):
                    out[block, side] = value
                else:
                    for half in range(2):

                        @pl.when(block >> 1 == half)
                        def _(half=half, block=block, side=side, value=value):
                            outs[half][block & 1, side] = value


def join_body(ids, up, down, first, second, up_out, down_out):
    middle = SHARD // 2
    up_out[:middle] = (up[:middle] + first[...].astype(f32)).astype(bf16)
    up_out[middle:] = up[middle:].astype(bf16)
    down_out[:middle] = down[:middle].astype(bf16)
    down_out[middle:] = (down[middle:] + second[...].astype(f32)).astype(bf16)


def rotate_body(rotated, ids, *refs):
    parts, (cosine, sine, out) = refs[:-3], refs[-3:]
    if len(parts) == 1:
        parts = [parts[0].at[source] for source in range(ROWS)]
    for block in range(ROWS):
        rows = slice(block * BLOCK, (block + 1) * BLOCK)
        total = parts[0][rows].astype(f32)
        for part in parts[1:]:
            total = total + part[rows].astype(f32)
        for half in range(2):
            span = slice(half * HEAD, (half + 1) * HEAD)
            value = total[:, span]
            if half < rotated:
                value = value * cosine[rows] + pltpu.roll(value, HEAD // 2, 1) * sine[rows]
            out[rows, span] = value.astype(bf16)


def key_shards(shard):
    plane, place = shard >> 2, shard & 3
    mirror = PLANE - 1 - place
    chosen = jnp.where(place < 2, plane - 2, plane)
    return (
        shard,
        shard - PLANE,
        (plane - 1) * PLANE + mirror,
        shard - 2 * PLANE,
        chosen * PLANE + mirror,
    )


def mask_values(ids, key_shard, keyval, masked):
    shard = ids[0]
    first = (shard >> 4) << 4
    count = jnp.where(key_shard >= first, live_of(ids, jnp.maximum(key_shard, 0)), 0)
    for start in range(0, SHARD, CHUNK):

        @pl.when(start < count)
        def _():
            alive = (
                lax.broadcasted_iota(jnp.int32, (CHUNK, HEAD), 0) + start < count
            )
            rows = slice(start, start + CHUNK)
            values = keyval[rows, HEAD:].astype(f32)
            masked[rows, :HEAD] = jnp.where(alive, values, 0.0).astype(bf16)
            masked[rows, HEAD:] = jnp.where(alive, 1.0, 0.0).astype(bf16)

    return count


def accumulate(query, query_shard, query_count, blocks, sums, fresh):
    for start in range(0, SHARD, CHUNK):
        tokens = slice(start, start + CHUNK)
        place = start // CHUNK

        @pl.when(start < query_count)
        def _(tokens=tokens, place=place):
            if fresh:
                for head in range(2):
                    sums[head, tokens] = jnp.zeros((CHUNK, 2 * HEAD), f32)
            for key_shard, count, keyval, masked in blocks:
                back = query_shard - key_shard
                chunks = (count + (CHUNK - 1)) // CHUNK
                low = jnp.where(back == 2 * PLANE, place, 0)
                high = jnp.where(back == 0, jnp.minimum(chunks, place + 1), chunks)
                high = jnp.where((back >= 0) & (back <= 2 * PLANE), high, 0)
                edge = (back == 0) | (back == 2 * PLANE)

                def step(chunk, carry, keyval=keyval, masked=masked, back=back, edge=edge):
                    rows = pl.ds(pl.multiple_of(chunk * CHUNK, CHUNK), CHUNK)

                    def work(with_mask):
                        keys = keyval[rows, :HEAD]
                        values = masked[rows, :]
                        if with_mask:
                            key_at = lax.broadcasted_iota(jnp.int32, (CHUNK, CHUNK), 1)
                            query_at = lax.broadcasted_iota(jnp.int32, (CHUNK, CHUNK), 0)
                            ahead = jnp.where(key_at <= query_at, 1, 0)
                            seen = ahead == jnp.where(back == 0, 1, 0)
                        for head in range(2):
                            scores = lax.dot_general(
                                query[tokens, head * HEAD : (head + 1) * HEAD],
                                keys,
                                (((1,), (1,)), ((), ())),
                                preferred_element_type=f32,
                            )
                            weights = jnp.exp2(jnp.tanh(scores * TO_TANH) * TO_EXP2)
                            if with_mask:
                                weights = jnp.where(seen, weights, 0.0)
                            sums[head, tokens] += jnp.dot(
                                weights.astype(bf16), values, preferred_element_type=f32
                            )

                    masked_step = edge & (chunk == place)

                    @pl.when(masked_step)
                    def _():
                        work(True)

                    @pl.when(jnp.logical_not(masked_step))
                    def _():
                        work(False)

                    return carry

                lax.fori_loop(low, high, step, 0)


def early_body(ids, query, own, back1, mirror1, back2, sums, *masked):
    shard, _, _ = scalars(ids)
    shards = key_shards(shard)
    held = (own, back1, mirror1, back2)
    blocks = [
        (shards[i], mask_values(ids, shards[i], held[i], masked[i]), held[i], masked[i])
        for i in range(len(held))
    ]
    accumulate(query, shard, live_of(ids, shard), blocks, sums, True)


def late_body(
    ids, query, pair, own, back1, mirror1, back2, chosen, before, out, sums, pair_sums, keys, values
):
    shard, _, _ = scalars(ids)
    side = shard & 1
    partner = shard + 1 - 2 * side
    own_shard, back1_shard, mirror1_shard, back2_shard, chosen_shard = key_shards(shard)
    first = (shard >> 4) << 4
    used = 0
    listed = (
        (own, own_shard, side == 0),
        (back2, back2_shard, side == 1),
        (back1, back1_shard, True),
        (mirror1, mirror1_shard, True),
        (chosen, chosen_shard, True),
    )
    for place, (keyval, key_shard, seen) in enumerate(listed):
        if place == 4:
            common = used
        counted = (key_shard >= first) & seen
        count = jnp.where(counted, live_of(ids, jnp.maximum(key_shard, 0)), 0)
        for start in range(0, SHARD, TILE):

            @pl.when(start < count)
            def _(keyval=keyval, start=start, used=used, count=count):
                alive = lax.broadcasted_iota(jnp.int32, (TILE, HEAD), 0) + start < count
                rows = pl.ds(pl.multiple_of(used * TILE + start, TILE), TILE)
                keys[rows, :] = keyval[start : start + TILE, :HEAD]
                value = keyval[start : start + TILE, HEAD:].astype(f32)
                values[rows, :HEAD] = jnp.where(alive, value, 0.0).astype(bf16)
                values[rows, HEAD:] = jnp.where(alive, 1.0, 0.0).astype(bf16)

        used = used + ((count + (TILE - 1)) >> 7)
    rows = pl.ds(pl.multiple_of(used * TILE, TILE), 3 * TILE)
    keys[rows, :] = jnp.zeros((3 * TILE, HEAD), bf16)
    values[rows, :] = jnp.zeros((3 * TILE, 2 * HEAD), bf16)

    def attend(query, live, low, width, sums):
        for start in range(0, SHARD, CHUNK):
            tokens = slice(start, start + CHUNK)

            @pl.when(start < live)
            def _(tokens=tokens):
                heads = [query[tokens, :HEAD], query[tokens, HEAD:]]
                stacked = jnp.concatenate(heads, 0)
                for head in range(2):
                    sums[head, tokens] = jnp.zeros((CHUNK, 2 * HEAD), f32)

                def step(index, carry):
                    at = pl.ds(pl.multiple_of((low + index * width) * TILE, TILE), width * TILE)
                    scores = lax.dot_general(
                        stacked, keys[at, :], (((1,), (1,)), ((), ())), preferred_element_type=f32
                    )
                    weights = jnp.exp2(jnp.tanh(scores * TO_TANH) * TO_EXP2).astype(bf16)
                    added = jnp.dot(weights, values[at, :], preferred_element_type=f32)
                    for head in range(2):
                        sums[head, tokens] += added[head * CHUNK : (head + 1) * CHUNK]
                    return carry

                lax.fori_loop(0, (used - low + (width - 1)) // width, step, 0)

    count, pair_count = live_of(ids, shard), live_of(ids, partner)
    attend(query, count, common, 2, sums)
    attend(pair, pair_count, 0, 4, pair_sums)
    same = lax.broadcasted_iota(jnp.int32, (BLOCK, HEAD), 0) == lax.broadcasted_iota(
        jnp.int32, (BLOCK, HEAD), 1
    )
    for held, live, owner, earlier in (
        (sums, count, side, before),
        (pair_sums, pair_count, 1 - side, None),
    ):
        for block in range(ROWS):
            start = block * BLOCK

            @pl.when(start < live)
            def _(held=held, owner=owner, earlier=earlier, block=block, start=start):
                target = owner * ROWS + block
                for head in range(2):
                    span = slice(head * HEAD, (head + 1) * HEAD)
                    total = held[head, start : start + BLOCK]
                    if earlier is not None:
                        total = total + earlier[head, start : start + BLOCK]
                    out[target, :BLOCK, span] = total[:, :HEAD].astype(bf16)
                    line = jnp.sum(jnp.where(same, total[:, HEAD:], 0.0), 0, keepdims=True)
                    line = jnp.broadcast_to(line, (8, HEAD))
                    coarse = line.astype(bf16).astype(f32)
                    out[target, BLOCK:, span] = jnp.concatenate([coarse, line - coarse], 0).astype(bf16)


def finish_body(ids, pieces, out):
    shard, row, _ = scalars(ids)
    at = lax.broadcasted_iota(jnp.int32, (BLOCK, HEAD), 0)
    same = at == lax.broadcasted_iota(jnp.int32, (BLOCK, HEAD), 1)
    alive = at + row * BLOCK < live_of(ids, shard)
    for group in range(ROWS):
        for head in range(2):
            span = slice(head * HEAD, (head + 1) * HEAD)
            numer = pieces[group, :BLOCK, span].astype(f32) + pieces[ROWS + group, :BLOCK, span].astype(f32)
            both = pieces[group, BLOCK:, span].astype(f32) + pieces[ROWS + group, BLOCK:, span].astype(f32)
            line = both[0:1] + both[8:9]
            denom = jnp.sum(jnp.where(same, line, 0.0), 1, keepdims=True)
            result = jnp.where(alive, numer * (1.0 / denom), 0.0)
            start = group * 2 * HEAD + head * HEAD
            out[:, start : start + HEAD] = result.astype(bf16)


def along_seq(value, target):
    pairs = []
    for shard in range(32):
        to = target(shard // PLANE, shard % PLANE)
        if to is not None:
            pairs.append((shard, to[0] * PLANE + to[1]))
    return lax.ppermute(value, SEQ, pairs)


def hop(value):
    planes = SEQ_SHARDS // PLANE
    return along_seq(value, lambda z, x: (z + 1, x) if z % planes != planes - 1 else None)


def mirrored(value):
    return along_seq(value, lambda z, x: (z, PLANE - 1 - x))


def turned(value):
    planes = SEQ_SHARDS // PLANE

    def target(z, x):
        if x < PLANE // 2:
            return z, PLANE - 1 - x
        return (z + 1, PLANE - 1 - x) if z % planes != planes - 1 else None

    return along_seq(value, target)


def paired(value):
    return along_seq(value, lambda z, x: (z, x ^ 1))


def onward(value, step):
    return lax.ppermute(value, "row", [(row, (row + step) % ROWS) for row in range(ROWS)])


def swapped(value):
    return lax.ppermute(value, "col", [(0, 1), (1, 0)])


def on_device(tokens, norm_gain, w_query, w_keyval, active):
    core = lax.axis_index("col")
    row = lax.axis_index("row")
    shard = lax.axis_index(SEQ)
    ids = jnp.concatenate([jnp.stack([shard, row, core]).astype(jnp.int32), active])
    sds = jax.ShapeDtypeStruct

    half_shape = sds((HALF, MODEL // 2), bf16)
    outgoing, kept = local(
        fetch_body,
        (tokens,),
        (half_shape, half_shape),
        "fetch",
        scratch=[pltpu.SemaphoreType.DMA((2,))],
        specs=[FAR],
    )
    received = swapped(outgoing)
    gain = norm_gain.reshape(1, MODEL)
    piece = sds((HALF, SLAB), bf16)
    normed = local(
        norm_body,
        (ids, kept, received, gain),
        [piece] * ROWS,
        "norm",
        scratch=[pltpu.VMEM((ROWS, HALF, SLAB), bf16)],
    )
    far_piece = onward(normed[2], 2)
    mine = [normed[0], onward(normed[1], 1), far_piece, onward(normed[3], 3)]
    theirs = [swapped(value) for value in mine]
    mine, place = lax.optimization_barrier((mine, shard))

    half = HEAD // 2
    positions = (place % SEQ_SHARDS) * SHARD + jnp.arange(SHARD, dtype=jnp.int32)
    freqs = 10000.0 ** (-2.0 * jnp.arange(half, dtype=f32) / HEAD)
    angles = positions.astype(f32)[:, None] * freqs[None, :]
    cosine, sine = jnp.cos(angles), jnp.sin(angles)
    cosine = jnp.concatenate([cosine, cosine], 1)
    sine = jnp.concatenate([-sine, sine], 1)

    flat = w_keyval.reshape(SLAB, 2 * ROWS * HEAD)
    held = sds((SHARD, 2 * HEAD), bf16)
    split = (ROWS, 2, HALF, 2 * HEAD)
    flops = 2 * SHARD * SLAB * 8 * HEAD

    def sums_across(mine, theirs, weights, split_columns, steps, kind, name, count=1):
        parts = local(
            functools.partial(partial_body, steps, split_columns),
            (ids, *mine, *theirs, weights),
            [sds((ROWS // count,) + split[1:], kind)] * (len(steps) * count),
            name,
            flops=flops * len(steps) // ROWS,
        )
        return [value.reshape(SHARD // count, 2 * HEAD) for value in parts]

    def joined(up, down, first, second, name):
        return local(join_body, (ids, up, down, first, second), [held, held], name)

    first, second = sums_across(mine, theirs, flat, True, (2,), bf16, "keyval_far", 2)
    mine, theirs, first, second = lax.optimization_barrier((mine, theirs, first, second))
    first, second = onward(first, 1), onward(second, 3)
    up, down, kept = sums_across(mine, theirs, flat, True, (1, 3, 0), f32, "keyval_near")
    mine, theirs, kept, cosine, sine = lax.optimization_barrier((mine, theirs, kept, cosine, sine))
    up, down = joined(up, down, first, second, "keyval_join")
    mine, theirs, up, down = lax.optimization_barrier((mine, theirs, up, down))
    up, down = onward(up, 1), onward(down, 3)
    steps = (2, 1, 3, 0)
    query_sums = sums_across(mine, theirs, w_query, False, steps, bf16, "query_partial")
    own = local(
        functools.partial(rotate_body, 1), (ids, kept, up, down, cosine, sine), held, "keyval_rotate"
    )
    query_sums, own = lax.optimization_barrier((query_sums, own))
    query_sums = [onward(value, step) if step else value for value, step in zip(query_sums, steps)]

    back1 = hop(own)
    back2 = hop(back1)
    mirror1 = mirrored(back1)
    chosen = turned(jnp.where(lax.axis_index("xh") == 0, own, back1))

    query_sums, back2 = lax.optimization_barrier((query_sums, back2))
    query = local(
        functools.partial(rotate_body, 2), (ids, *query_sums, cosine, sine), held, "query_rotate"
    )
    pair = paired(query)

    sums_shape = (2, SHARD, 2 * HEAD)
    masked = pltpu.VMEM((SHARD, 2 * HEAD), bf16)
    before = local(
        early_body,
        (ids, query, own, back1, mirror1, back2),
        sds(sums_shape, f32),
        "attend_early",
        scratch=[masked] * 4,
        flops=2**31,
    )
    pieces = local(
        late_body,
        (ids, query, pair, own, back1, mirror1, back2, chosen, before),
        sds((2 * ROWS, PIECE, 2 * HEAD), bf16),
        "attend_late",
        scratch=[
            pltpu.VMEM(sums_shape, f32),
            pltpu.VMEM(sums_shape, f32),
            pltpu.VMEM((LISTED, HEAD), bf16),
            pltpu.VMEM((LISTED, 2 * HEAD), bf16),
        ],
        flops=2**31,
        limit=16 * 2**20,
    )
    returned = lax.all_to_all(pieces, ("xl", "row"), 0, 0)
    return local(finish_body, (ids, returned), sds((BLOCK, ROWS * 2 * HEAD), bf16), "finish")


def solution(mesh):
    fine = Mesh(mesh.devices.reshape(8, 2, 2, ROWS, 2), SEQ + ("row", "col"))
    tokens_spec = P(SEQ + ("row",), "col")
    placed = (tokens_spec, P(), P("row", "col"), P("row", None, "col"), P())
    return jax.shard_map(
        on_device, mesh=fine, in_specs=placed, out_specs=tokens_spec, check_vma=False
    )
```

```python
import functools
import math

import jax
import jax.numpy as jnp
from jax import lax
from jax.experimental import pallas as pl
from jax.experimental.pallas import tpu as pltpu
from jax.sharding import Mesh, PartitionSpec as P

SCALE = 1.0 / 12.0
SOFTCAP = 50.0
EPSILON = 1e-06

HEAD = 128
SHARD = 512
SEQ_SHARDS = 16
PLANE = 4
ROWS = 4
BLOCK = SHARD // ROWS
HALF = BLOCK // 2
MODEL = 4608
SLAB = MODEL // ROWS
CHUNK = 256
TILE = 128
LISTED = 4 * SHARD + 4 * TILE
DEN_ROWS = 16
PIECE = BLOCK + DEN_ROWS
SEQ = ("z", "xh", "xl")

TO_TANH = SCALE / SOFTCAP
TO_EXP2 = SOFTCAP * math.log2(math.e)

bf16 = jnp.bfloat16
f32 = jnp.float32
VMEM = pl.BlockSpec(memory_space=pltpu.VMEM)
SMEM = pl.BlockSpec(memory_space=pltpu.SMEM)


def local(body, operands, out_shapes, name, scratch=(), flops=0, limit=8 * 2**20):
    return pl.pallas_call(
        body,
        out_shape=out_shapes,
        in_specs=[SMEM] + [VMEM] * (len(operands) - 1),
        out_specs=jax.tree.map(lambda _: VMEM, out_shapes),
        scratch_shapes=list(scratch),
        compiler_params=pltpu.CompilerParams(vmem_limit_bytes=limit),
        cost_estimate=pl.CostEstimate(flops=flops, bytes_accessed=2**20, transcendentals=0),
        name=name,
    )(*operands)


def scalars(ids):
    return ids[0], ids[1], ids[2]


def live_of(ids, shard):
    return ids[3 + shard]


def norm_body(ids, own, received, gain, *refs):
    outs, whole = refs[:ROWS], refs[ROWS]
    _, row, core = scalars(ids)
    kept = own[...].astype(f32)
    other = received[pl.ds(pl.multiple_of(core * HALF, HALF), HALF), :].astype(f32)
    total = jnp.sum(kept * kept, -1, keepdims=True) + jnp.sum(other * other, -1, keepdims=True)
    inverse = lax.rsqrt(total * (1.0 / MODEL) + EPSILON)
    for part in range(2):
        span = slice(part * SLAB, (part + 1) * SLAB)
        for value, slab in ((kept, 2 * core + part), (other, 2 * (1 - core) + part)):
            scale = gain[:, pl.ds(pl.multiple_of(slab * SLAB, HEAD), SLAB)]
            whole[slab] = (value[:, span] * inverse * scale).astype(bf16)
    for step in range(ROWS):
        outs[step][...] = whole[(row + step) & (ROWS - 1)]


def partial_body(steps, split, ids, *refs):
    mine, theirs, weights, outs = refs[:ROWS], refs[ROWS : 2 * ROWS], refs[2 * ROWS], refs[2 * ROWS + 1 :]
    _, row, core = scalars(ids)
    for step, out in zip(steps, outs):
        target = (row + step) & (ROWS - 1)
        if split:
            columns = [
                weights[:, pl.ds(pl.multiple_of((part * ROWS + target) * HEAD, HEAD), HEAD)]
                for part in range(2)
            ]
            columns = jnp.concatenate(columns, 1)
        else:
            columns = weights[:, pl.ds(pl.multiple_of(target * 2 * HEAD, 2 * HEAD), 2 * HEAD)]
        for pieces, side in ((mine, core), (theirs, 1 - core)):
            rows = jnp.concatenate([piece[...] for piece in pieces], 0)
            sums = jnp.dot(rows, columns, preferred_element_type=f32).astype(out.dtype)
            for back in range(ROWS):
                block = (row - back) & (ROWS - 1)
                value = sums[back * HALF : (back + 1) * HALF]
                if len(outs) == len(steps):
                    out[block, side] = value
                else:
                    for half in range(2):
                        outs[half][block, side] = value[:, half * HEAD : (half + 1) * HEAD]


def join_body(ids, up, down, first, second, up_out, down_out):
    up_out[:, :HEAD] = (up[:, :HEAD] + first[...].astype(f32)).astype(bf16)
    up_out[:, HEAD:] = up[:, HEAD:].astype(bf16)
    down_out[:, :HEAD] = down[:, :HEAD].astype(bf16)
    down_out[:, HEAD:] = (down[:, HEAD:] + second[...].astype(f32)).astype(bf16)


def rotate_body(rotated, ids, *refs):
    parts, (cosine, sine, out) = refs[:-3], refs[-3:]
    if len(parts) == 1:
        parts = [parts[0].at[source] for source in range(ROWS)]
    for block in range(ROWS):
        rows = slice(block * BLOCK, (block + 1) * BLOCK)
        total = parts[0][rows].astype(f32)
        for part in parts[1:]:
            total = total + part[rows].astype(f32)
        for half in range(2):
            span = slice(half * HEAD, (half + 1) * HEAD)
            value = total[:, span]
            if half < rotated:
                value = value * cosine[rows] + pltpu.roll(value, HEAD // 2, 1) * sine[rows]
            out[rows, span] = value.astype(bf16)


def key_shards(shard):
    plane, place = shard >> 2, shard & 3
    mirror = PLANE - 1 - place
    chosen = jnp.where(place < 2, plane - 2, plane)
    return (
        shard,
        shard - PLANE,
        (plane - 1) * PLANE + mirror,
        shard - 2 * PLANE,
        chosen * PLANE + mirror,
    )


def mask_values(ids, key_shard, keyval, masked):
    shard = ids[0]
    first = (shard >> 4) << 4
    count = jnp.where(key_shard >= first, live_of(ids, jnp.maximum(key_shard, 0)), 0)
    for start in range(0, SHARD, CHUNK):

        @pl.when(start < count)
        def _():
            alive = (
                lax.broadcasted_iota(jnp.int32, (CHUNK, HEAD), 0) + start < count
            )
            rows = slice(start, start + CHUNK)
            values = keyval[rows, HEAD:].astype(f32)
            masked[rows, :HEAD] = jnp.where(alive, values, 0.0).astype(bf16)
            masked[rows, HEAD:] = jnp.where(alive, 1.0, 0.0).astype(bf16)

    return count


def accumulate(query, query_shard, query_count, blocks, sums, fresh):
    for start in range(0, SHARD, CHUNK):
        tokens = slice(start, start + CHUNK)
        place = start // CHUNK

        @pl.when(start < query_count)
        def _(tokens=tokens, place=place):
            if fresh:
                for head in range(2):
                    sums[head, tokens] = jnp.zeros((CHUNK, 2 * HEAD), f32)
            for key_shard, count, keyval, masked in blocks:
                back = query_shard - key_shard
                chunks = (count + (CHUNK - 1)) // CHUNK
                low = jnp.where(back == 2 * PLANE, place, 0)
                high = jnp.where(back == 0, jnp.minimum(chunks, place + 1), chunks)
                high = jnp.where((back >= 0) & (back <= 2 * PLANE), high, 0)
                edge = (back == 0) | (back == 2 * PLANE)

                def step(chunk, carry, keyval=keyval, masked=masked, back=back, edge=edge):
                    rows = pl.ds(pl.multiple_of(chunk * CHUNK, CHUNK), CHUNK)

                    def work(with_mask):
                        keys = keyval[rows, :HEAD]
                        values = masked[rows, :]
                        if with_mask:
                            key_at = lax.broadcasted_iota(jnp.int32, (CHUNK, CHUNK), 1)
                            query_at = lax.broadcasted_iota(jnp.int32, (CHUNK, CHUNK), 0)
                            ahead = jnp.where(key_at <= query_at, 1, 0)
                            seen = ahead == jnp.where(back == 0, 1, 0)
                        for head in range(2):
                            scores = lax.dot_general(
                                query[tokens, head * HEAD : (head + 1) * HEAD],
                                keys,
                                (((1,), (1,)), ((), ())),
                                preferred_element_type=f32,
                            )
                            weights = jnp.exp2(jnp.tanh(scores * TO_TANH) * TO_EXP2)
                            if with_mask:
                                weights = jnp.where(seen, weights, 0.0)
                            sums[head, tokens] += jnp.dot(
                                weights.astype(bf16), values, preferred_element_type=f32
                            )

                    masked_step = edge & (chunk == place)

                    @pl.when(masked_step)
                    def _():
                        work(True)

                    @pl.when(jnp.logical_not(masked_step))
                    def _():
                        work(False)

                    return carry

                lax.fori_loop(low, high, step, 0)


def early_body(ids, query, own, back1, mirror1, back2, sums, *masked):
    shard, _, _ = scalars(ids)
    shards = key_shards(shard)
    held = (own, back1, mirror1, back2)
    blocks = [
        (shards[i], mask_values(ids, shards[i], held[i], masked[i]), held[i], masked[i])
        for i in range(len(held))
    ]
    accumulate(query, shard, live_of(ids, shard), blocks, sums, True)


def late_body(
    ids, query, pair, own, back1, mirror1, back2, chosen, before, out, sums, pair_sums, keys, values
):
    shard, _, _ = scalars(ids)
    side = shard & 1
    partner = shard + 1 - 2 * side
    own_shard, back1_shard, mirror1_shard, back2_shard, chosen_shard = key_shards(shard)
    first = (shard >> 4) << 4
    used = 0
    listed = (
        (own, own_shard, side == 0),
        (back2, back2_shard, side == 1),
        (back1, back1_shard, True),
        (mirror1, mirror1_shard, True),
        (chosen, chosen_shard, True),
    )
    for place, (keyval, key_shard, seen) in enumerate(listed):
        if place == 4:
            common = used
        counted = (key_shard >= first) & seen
        count = jnp.where(counted, live_of(ids, jnp.maximum(key_shard, 0)), 0)
        for start in range(0, SHARD, TILE):

            @pl.when(start < count)
            def _(keyval=keyval, start=start, used=used, count=count):
                alive = lax.broadcasted_iota(jnp.int32, (TILE, HEAD), 0) + start < count
                rows = pl.ds(pl.multiple_of(used * TILE + start, TILE), TILE)
                keys[rows, :] = keyval[start : start + TILE, :HEAD]
                value = keyval[start : start + TILE, HEAD:].astype(f32)
                values[rows, :HEAD] = jnp.where(alive, value, 0.0).astype(bf16)
                values[rows, HEAD:] = jnp.where(alive, 1.0, 0.0).astype(bf16)

        used = used + ((count + (TILE - 1)) >> 7)
    rows = pl.ds(pl.multiple_of(used * TILE, TILE), 3 * TILE)
    keys[rows, :] = jnp.zeros((3 * TILE, HEAD), bf16)
    values[rows, :] = jnp.zeros((3 * TILE, 2 * HEAD), bf16)

    def attend(query, live, low, width, sums):
        for start in range(0, SHARD, CHUNK):
            tokens = slice(start, start + CHUNK)

            @pl.when(start < live)
            def _(tokens=tokens):
                heads = [query[tokens, :HEAD], query[tokens, HEAD:]]
                stacked = jnp.concatenate(heads, 0)
                for head in range(2):
                    sums[head, tokens] = jnp.zeros((CHUNK, 2 * HEAD), f32)

                def step(index, carry):
                    at = pl.ds(pl.multiple_of((low + index * width) * TILE, TILE), width * TILE)
                    scores = lax.dot_general(
                        stacked, keys[at, :], (((1,), (1,)), ((), ())), preferred_element_type=f32
                    )
                    weights = jnp.exp2(jnp.tanh(scores * TO_TANH) * TO_EXP2).astype(bf16)
                    added = jnp.dot(weights, values[at, :], preferred_element_type=f32)
                    for head in range(2):
                        sums[head, tokens] += added[head * CHUNK : (head + 1) * CHUNK]
                    return carry

                lax.fori_loop(0, (used - low + (width - 1)) // width, step, 0)

    count, pair_count = live_of(ids, shard), live_of(ids, partner)
    attend(query, count, common, 2, sums)
    attend(pair, pair_count, 0, 4, pair_sums)
    same = lax.broadcasted_iota(jnp.int32, (BLOCK, HEAD), 0) == lax.broadcasted_iota(
        jnp.int32, (BLOCK, HEAD), 1
    )
    for held, live, owner, earlier in (
        (sums, count, side, before),
        (pair_sums, pair_count, 1 - side, None),
    ):
        for block in range(ROWS):
            start = block * BLOCK

            @pl.when(start < live)
            def _(held=held, owner=owner, earlier=earlier, block=block, start=start):
                target = owner * ROWS + block
                for head in range(2):
                    span = slice(head * HEAD, (head + 1) * HEAD)
                    total = held[head, start : start + BLOCK]
                    if earlier is not None:
                        total = total + earlier[head, start : start + BLOCK]
                    out[target, :BLOCK, span] = total[:, :HEAD].astype(bf16)
                    line = jnp.sum(jnp.where(same, total[:, HEAD:], 0.0), 0, keepdims=True)
                    line = jnp.broadcast_to(line, (8, HEAD))
                    coarse = line.astype(bf16).astype(f32)
                    out[target, BLOCK:, span] = jnp.concatenate([coarse, line - coarse], 0).astype(bf16)


def finish_body(ids, pieces, out):
    shard, row, _ = scalars(ids)
    at = lax.broadcasted_iota(jnp.int32, (BLOCK, HEAD), 0)
    same = at == lax.broadcasted_iota(jnp.int32, (BLOCK, HEAD), 1)
    alive = at + row * BLOCK < live_of(ids, shard)
    for group in range(ROWS):
        for head in range(2):
            span = slice(head * HEAD, (head + 1) * HEAD)
            numer = pieces[group, :BLOCK, span].astype(f32) + pieces[ROWS + group, :BLOCK, span].astype(f32)
            both = pieces[group, BLOCK:, span].astype(f32) + pieces[ROWS + group, BLOCK:, span].astype(f32)
            line = both[0:1] + both[8:9]
            denom = jnp.sum(jnp.where(same, line, 0.0), 1, keepdims=True)
            result = jnp.where(alive, numer * (1.0 / denom), 0.0)
            start = group * 2 * HEAD + head * HEAD
            out[:, start : start + HEAD] = result.astype(bf16)


def along_seq(value, target):
    pairs = []
    for shard in range(32):
        to = target(shard // PLANE, shard % PLANE)
        if to is not None:
            pairs.append((shard, to[0] * PLANE + to[1]))
    return lax.ppermute(value, SEQ, pairs)


def hop(value):
    planes = SEQ_SHARDS // PLANE
    return along_seq(value, lambda z, x: (z + 1, x) if z % planes != planes - 1 else None)


def mirrored(value):
    return along_seq(value, lambda z, x: (z, PLANE - 1 - x))


def turned(value):
    planes = SEQ_SHARDS // PLANE

    def target(z, x):
        if x < PLANE // 2:
            return z, PLANE - 1 - x
        return (z + 1, PLANE - 1 - x) if z % planes != planes - 1 else None

    return along_seq(value, target)


def paired(value):
    return along_seq(value, lambda z, x: (z, x ^ 1))


def onward(value, step):
    return lax.ppermute(value, "row", [(row, (row + step) % ROWS) for row in range(ROWS)])


def swapped(value):
    return lax.ppermute(value, "col", [(0, 1), (1, 0)])


def on_device(tokens, norm_gain, w_query, w_keyval, active):
    core = lax.axis_index("col")
    row = lax.axis_index("row")
    shard = lax.axis_index(SEQ)
    ids = jnp.concatenate([jnp.stack([shard, row, core]).astype(jnp.int32), active])
    sds = jax.ShapeDtypeStruct

    received = swapped(tokens)
    kept = lax.dynamic_slice_in_dim(tokens, core * HALF, HALF, 0)
    gain = norm_gain.reshape(1, MODEL)
    piece = sds((HALF, SLAB), bf16)
    normed = local(
        norm_body,
        (ids, kept, received, gain),
        [piece] * ROWS,
        "norm",
        scratch=[pltpu.VMEM((ROWS, HALF, SLAB), bf16)],
    )
    far_piece = onward(normed[2], 2)
    mine = [normed[0], onward(normed[1], 1), far_piece, onward(normed[3], 3)]
    theirs = [swapped(value) for value in mine]
    mine, place = lax.optimization_barrier((mine, shard))

    half = HEAD // 2
    positions = (place % SEQ_SHARDS) * SHARD + jnp.arange(SHARD, dtype=jnp.int32)
    freqs = 10000.0 ** (-2.0 * jnp.arange(half, dtype=f32) / HEAD)
    angles = positions.astype(f32)[:, None] * freqs[None, :]
    cosine, sine = jnp.cos(angles), jnp.sin(angles)
    cosine = jnp.concatenate([cosine, cosine], 1)
    sine = jnp.concatenate([-sine, sine], 1)

    flat = w_keyval.reshape(SLAB, 2 * ROWS * HEAD)
    held = sds((SHARD, 2 * HEAD), bf16)
    split = (ROWS, 2, HALF, 2 * HEAD)
    flops = 2 * SHARD * SLAB * 8 * HEAD

    def sums_across(mine, theirs, weights, split_columns, steps, kind, name, count=1):
        parts = local(
            functools.partial(partial_body, steps, split_columns),
            (ids, *mine, *theirs, weights),
            [sds(split[:3] + (2 * HEAD // count,), kind)] * (len(steps) * count),
            name,
            flops=flops * len(steps) // ROWS,
        )
        return [value.reshape(SHARD, 2 * HEAD // count) for value in parts]

    def joined(up, down, first, second, name):
        return local(join_body, (ids, up, down, first, second), [held, held], name)

    first, second = sums_across(mine, theirs, flat, True, (2,), bf16, "keyval_far", 2)
    mine, theirs, first, second = lax.optimization_barrier((mine, theirs, first, second))
    first, second = onward(first, 1), onward(second, 3)
    up, down, kept = sums_across(mine, theirs, flat, True, (1, 3, 0), f32, "keyval_near")
    mine, theirs, kept, cosine, sine = lax.optimization_barrier((mine, theirs, kept, cosine, sine))
    up, down = joined(up, down, first, second, "keyval_join")
    mine, theirs, up, down = lax.optimization_barrier((mine, theirs, up, down))
    up, down = onward(up, 1), onward(down, 3)
    steps = (2, 1, 3, 0)
    query_sums = sums_across(mine, theirs, w_query, False, steps, bf16, "query_partial")
    own = local(
        functools.partial(rotate_body, 1), (ids, kept, up, down, cosine, sine), held, "keyval_rotate"
    )
    query_sums, own = lax.optimization_barrier((query_sums, own))
    query_sums = [onward(value, step) if step else value for value, step in zip(query_sums, steps)]

    back1 = hop(own)
    back2 = hop(back1)
    mirror1 = mirrored(back1)
    chosen = turned(jnp.where(lax.axis_index("xh") == 0, own, back1))

    query_sums, back2 = lax.optimization_barrier((query_sums, back2))
    query = local(
        functools.partial(rotate_body, 2), (ids, *query_sums, cosine, sine), held, "query_rotate"
    )
    pair = paired(query)

    sums_shape = (2, SHARD, 2 * HEAD)
    masked = pltpu.VMEM((SHARD, 2 * HEAD), bf16)
    before = local(
        early_body,
        (ids, query, own, back1, mirror1, back2),
        sds(sums_shape, f32),
        "attend_early",
        scratch=[masked] * 4,
        flops=2**31,
    )
    pieces = local(
        late_body,
        (ids, query, pair, own, back1, mirror1, back2, chosen, before),
        sds((2 * ROWS, PIECE, 2 * HEAD), bf16),
        "attend_late",
        scratch=[
            pltpu.VMEM(sums_shape, f32),
            pltpu.VMEM(sums_shape, f32),
            pltpu.VMEM((LISTED, HEAD), bf16),
            pltpu.VMEM((LISTED, 2 * HEAD), bf16),
        ],
        flops=2**31,
        limit=16 * 2**20,
    )
    returned = lax.all_to_all(pieces, ("xl", "row"), 0, 0)
    return local(finish_body, (ids, returned), sds((BLOCK, ROWS * 2 * HEAD), bf16), "finish")


def solution(mesh):
    fine = Mesh(mesh.devices.reshape(8, 2, 2, ROWS, 2), SEQ + ("row", "col"))
    tokens_spec = P(SEQ + ("row",), "col")
    placed = (tokens_spec, P(), P("row", "col"), P("row", None, "col"), P())
    return jax.shard_map(
        on_device, mesh=fine, in_specs=placed, out_specs=tokens_spec, check_vma=False
    )
```

```python
import functools
import math

import jax
import jax.numpy as jnp
from jax import lax
from jax.experimental import pallas as pl
from jax.experimental.pallas import tpu as pltpu
from jax.sharding import Mesh, PartitionSpec as P

SCALE = 1.0 / 12.0
SOFTCAP = 50.0
EPSILON = 1e-06

HEAD = 128
SHARD = 512
SEQ_SHARDS = 16
PLANE = 4
ROWS = 4
BLOCK = SHARD // ROWS
HALF = BLOCK // 2
MODEL = 4608
SLAB = MODEL // ROWS
CHUNK = 256
TILE = 128
LISTED = 4 * SHARD + 4 * TILE
DEN_ROWS = 16
PIECE = BLOCK + DEN_ROWS
SEQ = ("z", "xh", "xl")

TO_TANH = SCALE / SOFTCAP
TO_EXP2 = SOFTCAP * math.log2(math.e)

bf16 = jnp.bfloat16
f32 = jnp.float32
VMEM = pl.BlockSpec(memory_space=pltpu.VMEM)
SMEM = pl.BlockSpec(memory_space=pltpu.SMEM)


def local(body, operands, out_shapes, name, scratch=(), flops=0, limit=8 * 2**20):
    return pl.pallas_call(
        body,
        out_shape=out_shapes,
        in_specs=[SMEM] + [VMEM] * (len(operands) - 1),
        out_specs=jax.tree.map(lambda _: VMEM, out_shapes),
        scratch_shapes=list(scratch),
        compiler_params=pltpu.CompilerParams(vmem_limit_bytes=limit),
        cost_estimate=pl.CostEstimate(flops=flops, bytes_accessed=2**20, transcendentals=0),
        name=name,
    )(*operands)


def scalars(ids):
    return ids[0], ids[1], ids[2]


def live_of(ids, shard):
    return ids[3 + shard]


def norm_body(ids, own, received, gain, *refs):
    outs, whole = refs[:ROWS], refs[ROWS]
    _, row, core = scalars(ids)
    kept = own[...].astype(f32)
    other = received[pl.ds(pl.multiple_of(core * HALF, HALF), HALF), :].astype(f32)
    total = jnp.sum(kept * kept, -1, keepdims=True) + jnp.sum(other * other, -1, keepdims=True)
    inverse = lax.rsqrt(total * (1.0 / MODEL) + EPSILON)
    for part in range(2):
        span = slice(part * SLAB, (part + 1) * SLAB)
        for value, slab in ((kept, 2 * core + part), (other, 2 * (1 - core) + part)):
            scale = gain[:, pl.ds(pl.multiple_of(slab * SLAB, HEAD), SLAB)]
            whole[slab] = (value[:, span] * inverse * scale).astype(bf16)
    for step in range(ROWS):
        outs[step][...] = whole[(row + step) & (ROWS - 1)]


def partial_body(steps, split, ids, *refs):
    mine, theirs, weights, outs = refs[:ROWS], refs[ROWS : 2 * ROWS], refs[2 * ROWS], refs[2 * ROWS + 1 :]
    _, row, core = scalars(ids)
    for step, out in zip(steps, outs):
        target = (row + step) & (ROWS - 1)
        if split:
            columns = [
                weights[:, pl.ds(pl.multiple_of((part * ROWS + target) * HEAD, HEAD), HEAD)]
                for part in range(2)
            ]
            columns = jnp.concatenate(columns, 1)
        else:
            columns = weights[:, pl.ds(pl.multiple_of(target * 2 * HEAD, 2 * HEAD), 2 * HEAD)]
        for pieces, side in ((mine, core), (theirs, 1 - core)):
            rows = jnp.concatenate([piece[...] for piece in pieces], 0)
            sums = jnp.dot(rows, columns, preferred_element_type=f32).astype(out.dtype)
            for back in range(ROWS):
                block = (row - back) & (ROWS - 1)
                value = sums[back * HALF : (back + 1) * HALF]
                if len(outs) == len(steps):
                    out[block, side] = value
                else:
                    for half in range(2):
                        outs[half][block, side] = value[:, half * HEAD : (half + 1) * HEAD]


def join_body(ids, up, down, first, second, up_out, down_out):
    up_out[:, :HEAD] = (up[:, :HEAD] + first[...].astype(f32)).astype(bf16)
    up_out[:, HEAD:] = up[:, HEAD:].astype(bf16)
    down_out[:, :HEAD] = down[:, :HEAD].astype(bf16)
    down_out[:, HEAD:] = (down[:, HEAD:] + second[...].astype(f32)).astype(bf16)


def rotate_body(rotated, ids, *refs):
    parts, (cosine, sine, out) = refs[:-3], refs[-3:]
    if len(parts) == 1:
        parts = [parts[0].at[source] for source in range(ROWS)]
    for block in range(ROWS):
        rows = slice(block * BLOCK, (block + 1) * BLOCK)
        total = parts[0][rows].astype(f32)
        for part in parts[1:]:
            total = total + part[rows].astype(f32)
        for half in range(2):
            span = slice(half * HEAD, (half + 1) * HEAD)
            value = total[:, span]
            if half < rotated:
                value = value * cosine[rows] + pltpu.roll(value, HEAD // 2, 1) * sine[rows]
            out[rows, span] = value.astype(bf16)


def key_shards(shard):
    plane, place = shard >> 2, shard & 3
    mirror = PLANE - 1 - place
    chosen = jnp.where(place < 2, plane - 2, plane)
    return (
        shard,
        shard - PLANE,
        (plane - 1) * PLANE + mirror,
        shard - 2 * PLANE,
        chosen * PLANE + mirror,
    )


def mask_values(ids, key_shard, keyval, masked):
    shard = ids[0]
    first = (shard >> 4) << 4
    count = jnp.where(key_shard >= first, live_of(ids, jnp.maximum(key_shard, 0)), 0)
    for start in range(0, SHARD, CHUNK):

        @pl.when(start < count)
        def _():
            alive = (
                lax.broadcasted_iota(jnp.int32, (CHUNK, HEAD), 0) + start < count
            )
            rows = slice(start, start + CHUNK)
            values = keyval[rows, HEAD:].astype(f32)
            masked[rows, :HEAD] = jnp.where(alive, values, 0.0).astype(bf16)
            masked[rows, HEAD:] = jnp.where(alive, 1.0, 0.0).astype(bf16)

    return count


def accumulate(query, query_shard, query_count, blocks, sums, fresh):
    for start in range(0, SHARD, CHUNK):
        tokens = slice(start, start + CHUNK)
        place = start // CHUNK

        @pl.when(start < query_count)
        def _(tokens=tokens, place=place):
            if fresh:
                for head in range(2):
                    sums[head, tokens] = jnp.zeros((CHUNK, 2 * HEAD), f32)
            for key_shard, count, keyval, masked in blocks:
                back = query_shard - key_shard
                chunks = (count + (CHUNK - 1)) // CHUNK
                low = jnp.where(back == 2 * PLANE, place, 0)
                high = jnp.where(back == 0, jnp.minimum(chunks, place + 1), chunks)
                high = jnp.where((back >= 0) & (back <= 2 * PLANE), high, 0)
                edge = (back == 0) | (back == 2 * PLANE)

                def step(chunk, carry, keyval=keyval, masked=masked, back=back, edge=edge):
                    rows = pl.ds(pl.multiple_of(chunk * CHUNK, CHUNK), CHUNK)

                    def work(with_mask):
                        keys = keyval[rows, :HEAD]
                        values = masked[rows, :]
                        if with_mask:
                            key_at = lax.broadcasted_iota(jnp.int32, (CHUNK, CHUNK), 1)
                            query_at = lax.broadcasted_iota(jnp.int32, (CHUNK, CHUNK), 0)
                            ahead = jnp.where(key_at <= query_at, 1, 0)
                            seen = ahead == jnp.where(back == 0, 1, 0)
                        for head in range(2):
                            scores = lax.dot_general(
                                query[tokens, head * HEAD : (head + 1) * HEAD],
                                keys,
                                (((1,), (1,)), ((), ())),
                                preferred_element_type=f32,
                            )
                            weights = jnp.exp2(jnp.tanh(scores * TO_TANH) * TO_EXP2)
                            if with_mask:
                                weights = jnp.where(seen, weights, 0.0)
                            sums[head, tokens] += jnp.dot(
                                weights.astype(bf16), values, preferred_element_type=f32
                            )

                    masked_step = edge & (chunk == place)

                    @pl.when(masked_step)
                    def _():
                        work(True)

                    @pl.when(jnp.logical_not(masked_step))
                    def _():
                        work(False)

                    return carry

                lax.fori_loop(low, high, step, 0)


def early_body(ids, query, own, back1, back2, sums, *masked):
    shard, _, _ = scalars(ids)
    shards = key_shards(shard)
    held = (own, back1, back2)
    shards = (shards[0], shards[1], shards[3])
    blocks = [
        (shards[i], mask_values(ids, shards[i], held[i], masked[i]), held[i], masked[i])
        for i in range(len(held))
    ]
    accumulate(query, shard, live_of(ids, shard), blocks, sums, True)


def late_body(
    ids, query, pair, own, back1, mirror1, back2, chosen, before, out, sums, pair_sums, keys, values
):
    shard, _, _ = scalars(ids)
    side = shard & 1
    partner = shard + 1 - 2 * side
    own_shard, back1_shard, mirror1_shard, back2_shard, chosen_shard = key_shards(shard)
    first = (shard >> 4) << 4
    used = 0
    listed = (
        (own, own_shard, side == 0),
        (back2, back2_shard, side == 1),
        (back1, back1_shard, True),
        (mirror1, mirror1_shard, True),
        (chosen, chosen_shard, True),
    )
    for place, (keyval, key_shard, seen) in enumerate(listed):
        if place == 3:
            common = used
        counted = (key_shard >= first) & seen
        count = jnp.where(counted, live_of(ids, jnp.maximum(key_shard, 0)), 0)
        for start in range(0, SHARD, TILE):

            @pl.when(start < count)
            def _(keyval=keyval, start=start, used=used, count=count):
                alive = lax.broadcasted_iota(jnp.int32, (TILE, HEAD), 0) + start < count
                rows = pl.ds(pl.multiple_of(used * TILE + start, TILE), TILE)
                keys[rows, :] = keyval[start : start + TILE, :HEAD]
                value = keyval[start : start + TILE, HEAD:].astype(f32)
                values[rows, :HEAD] = jnp.where(alive, value, 0.0).astype(bf16)
                values[rows, HEAD:] = jnp.where(alive, 1.0, 0.0).astype(bf16)

        used = used + ((count + (TILE - 1)) >> 7)
    rows = pl.ds(pl.multiple_of(used * TILE, TILE), 3 * TILE)
    keys[rows, :] = jnp.zeros((3 * TILE, HEAD), bf16)
    values[rows, :] = jnp.zeros((3 * TILE, 2 * HEAD), bf16)

    def attend(query, live, low, width, sums):
        for start in range(0, SHARD, CHUNK):
            tokens = slice(start, start + CHUNK)

            @pl.when(start < live)
            def _(tokens=tokens):
                heads = [query[tokens, :HEAD], query[tokens, HEAD:]]
                stacked = jnp.concatenate(heads, 0)
                for head in range(2):
                    sums[head, tokens] = jnp.zeros((CHUNK, 2 * HEAD), f32)

                def step(index, carry):
                    at = pl.ds(pl.multiple_of((low + index * width) * TILE, TILE), width * TILE)
                    scores = lax.dot_general(
                        stacked, keys[at, :], (((1,), (1,)), ((), ())), preferred_element_type=f32
                    )
                    weights = jnp.exp2(jnp.tanh(scores * TO_TANH) * TO_EXP2).astype(bf16)
                    added = jnp.dot(weights, values[at, :], preferred_element_type=f32)
                    for head in range(2):
                        sums[head, tokens] += added[head * CHUNK : (head + 1) * CHUNK]
                    return carry

                lax.fori_loop(0, (used - low + (width - 1)) // width, step, 0)

    count, pair_count = live_of(ids, shard), live_of(ids, partner)
    attend(query, count, common, 4, sums)
    attend(pair, pair_count, 0, 4, pair_sums)
    same = lax.broadcasted_iota(jnp.int32, (BLOCK, HEAD), 0) == lax.broadcasted_iota(
        jnp.int32, (BLOCK, HEAD), 1
    )
    for held, live, owner, earlier in (
        (sums, count, side, before),
        (pair_sums, pair_count, 1 - side, None),
    ):
        for block in range(ROWS):
            start = block * BLOCK

            @pl.when(start < live)
            def _(held=held, owner=owner, earlier=earlier, block=block, start=start):
                target = owner * ROWS + block
                for head in range(2):
                    span = slice(head * HEAD, (head + 1) * HEAD)
                    total = held[head, start : start + BLOCK]
                    if earlier is not None:
                        total = total + earlier[head, start : start + BLOCK]
                    out[target, :BLOCK, span] = total[:, :HEAD].astype(bf16)
                    line = jnp.sum(jnp.where(same, total[:, HEAD:], 0.0), 0, keepdims=True)
                    line = jnp.broadcast_to(line, (8, HEAD))
                    coarse = line.astype(bf16).astype(f32)
                    out[target, BLOCK:, span] = jnp.concatenate([coarse, line - coarse], 0).astype(bf16)


def finish_body(ids, pieces, out):
    shard, row, _ = scalars(ids)
    at = lax.broadcasted_iota(jnp.int32, (BLOCK, HEAD), 0)
    same = at == lax.broadcasted_iota(jnp.int32, (BLOCK, HEAD), 1)
    alive = at + row * BLOCK < live_of(ids, shard)
    for group in range(ROWS):
        for head in range(2):
            span = slice(head * HEAD, (head + 1) * HEAD)
            numer = pieces[group, :BLOCK, span].astype(f32) + pieces[ROWS + group, :BLOCK, span].astype(f32)
            both = pieces[group, BLOCK:, span].astype(f32) + pieces[ROWS + group, BLOCK:, span].astype(f32)
            line = both[0:1] + both[8:9]
            denom = jnp.sum(jnp.where(same, line, 0.0), 1, keepdims=True)
            result = jnp.where(alive, numer * (1.0 / denom), 0.0)
            start = group * 2 * HEAD + head * HEAD
            out[:, start : start + HEAD] = result.astype(bf16)


def along_seq(value, target):
    pairs = []
    for shard in range(32):
        to = target(shard // PLANE, shard % PLANE)
        if to is not None:
            pairs.append((shard, to[0] * PLANE + to[1]))
    return lax.ppermute(value, SEQ, pairs)


def hop(value):
    planes = SEQ_SHARDS // PLANE
    return along_seq(value, lambda z, x: (z + 1, x) if z % planes != planes - 1 else None)


def mirrored(value):
    return along_seq(value, lambda z, x: (z, PLANE - 1 - x))


def turned(value):
    planes = SEQ_SHARDS // PLANE

    def target(z, x):
        if x < PLANE // 2:
            return z, PLANE - 1 - x
        return (z + 1, PLANE - 1 - x) if z % planes != planes - 1 else None

    return along_seq(value, target)


def paired(value):
    return along_seq(value, lambda z, x: (z, x ^ 1))


def onward(value, step):
    return lax.ppermute(value, "row", [(row, (row + step) % ROWS) for row in range(ROWS)])


def swapped(value):
    return lax.ppermute(value, "col", [(0, 1), (1, 0)])


def on_device(tokens, norm_gain, w_query, w_keyval, active):
    core = lax.axis_index("col")
    row = lax.axis_index("row")
    shard = lax.axis_index(SEQ)
    ids = jnp.concatenate([jnp.stack([shard, row, core]).astype(jnp.int32), active])
    sds = jax.ShapeDtypeStruct

    received = swapped(tokens)
    kept = lax.dynamic_slice_in_dim(tokens, core * HALF, HALF, 0)
    gain = norm_gain.reshape(1, MODEL)
    piece = sds((HALF, SLAB), bf16)
    normed = local(
        norm_body,
        (ids, kept, received, gain),
        [piece] * ROWS,
        "norm",
        scratch=[pltpu.VMEM((ROWS, HALF, SLAB), bf16)],
    )
    far_piece = onward(normed[2], 2)
    mine = [normed[0], onward(normed[1], 1), far_piece, onward(normed[3], 3)]
    theirs = [swapped(value) for value in mine]
    mine, place = lax.optimization_barrier((mine, shard))

    half = HEAD // 2
    positions = (place % SEQ_SHARDS) * SHARD + jnp.arange(SHARD, dtype=jnp.int32)
    freqs = 10000.0 ** (-2.0 * jnp.arange(half, dtype=f32) / HEAD)
    angles = positions.astype(f32)[:, None] * freqs[None, :]
    cosine, sine = jnp.cos(angles), jnp.sin(angles)
    cosine = jnp.concatenate([cosine, cosine], 1)
    sine = jnp.concatenate([-sine, sine], 1)

    flat = w_keyval.reshape(SLAB, 2 * ROWS * HEAD)
    held = sds((SHARD, 2 * HEAD), bf16)
    split = (ROWS, 2, HALF, 2 * HEAD)
    flops = 2 * SHARD * SLAB * 8 * HEAD

    def sums_across(mine, theirs, weights, split_columns, steps, kind, name, count=1):
        parts = local(
            functools.partial(partial_body, steps, split_columns),
            (ids, *mine, *theirs, weights),
            [sds(split[:3] + (2 * HEAD // count,), kind)] * (len(steps) * count),
            name,
            flops=flops * len(steps) // ROWS,
        )
        return [value.reshape(SHARD, 2 * HEAD // count) for value in parts]

    def joined(up, down, first, second, name):
        return local(join_body, (ids, up, down, first, second), [held, held], name)

    first, second = sums_across(mine, theirs, flat, True, (2,), bf16, "keyval_far", 2)
    mine, theirs, first, second = lax.optimization_barrier((mine, theirs, first, second))
    first, second = onward(first, 1), onward(second, 3)
    up, down, kept = sums_across(mine, theirs, flat, True, (1, 3, 0), f32, "keyval_near")
    mine, theirs, kept, cosine, sine = lax.optimization_barrier((mine, theirs, kept, cosine, sine))
    up, down = joined(up, down, first, second, "keyval_join")
    mine, theirs, up, down = lax.optimization_barrier((mine, theirs, up, down))
    up, down = onward(up, 1), onward(down, 3)
    steps = (2, 1, 3, 0)
    query_sums = sums_across(mine, theirs, w_query, False, steps, bf16, "query_partial")
    own = local(
        functools.partial(rotate_body, 1), (ids, kept, up, down, cosine, sine), held, "keyval_rotate"
    )
    query_sums, own = lax.optimization_barrier((query_sums, own))
    query_sums = [onward(value, step) if step else value for value, step in zip(query_sums, steps)]

    back1 = hop(own)
    back2 = hop(back1)
    mirror1 = mirrored(back1)
    chosen = turned(jnp.where(lax.axis_index("xh") == 0, own, back1))

    query_sums, back2 = lax.optimization_barrier((query_sums, back2))
    query = local(
        functools.partial(rotate_body, 2), (ids, *query_sums, cosine, sine), held, "query_rotate"
    )
    pair = paired(query)

    sums_shape = (2, SHARD, 2 * HEAD)
    masked = pltpu.VMEM((SHARD, 2 * HEAD), bf16)
    before = local(
        early_body,
        (ids, query, own, back1, back2),
        sds(sums_shape, f32),
        "attend_early",
        scratch=[masked] * 3,
        flops=2**31,
    )
    pieces = local(
        late_body,
        (ids, query, pair, own, back1, mirror1, back2, chosen, before),
        sds((2 * ROWS, PIECE, 2 * HEAD), bf16),
        "attend_late",
        scratch=[
            pltpu.VMEM(sums_shape, f32),
            pltpu.VMEM(sums_shape, f32),
            pltpu.VMEM((LISTED, HEAD), bf16),
            pltpu.VMEM((LISTED, 2 * HEAD), bf16),
        ],
        flops=2**31,
        limit=16 * 2**20,
    )
    returned = lax.all_to_all(pieces, ("xl", "row"), 0, 0)
    return local(finish_body, (ids, returned), sds((BLOCK, ROWS * 2 * HEAD), bf16), "finish")


def solution(mesh):
    fine = Mesh(mesh.devices.reshape(8, 2, 2, ROWS, 2), SEQ + ("row", "col"))
    tokens_spec = P(SEQ + ("row",), "col")
    placed = (tokens_spec, P(), P("row", "col"), P("row", None, "col"), P())
    return jax.shard_map(
        on_device, mesh=fine, in_specs=placed, out_specs=tokens_spec, check_vma=False
    )
```

```python
import functools
import math

import jax
import jax.numpy as jnp
from jax import lax
from jax.experimental import pallas as pl
from jax.experimental.pallas import tpu as pltpu
from jax.sharding import Mesh, PartitionSpec as P

SCALE = 1.0 / 12.0
SOFTCAP = 50.0
EPSILON = 1e-06

HEAD = 128
SHARD = 512
SEQ_SHARDS = 16
PLANE = 4
ROWS = 4
BLOCK = SHARD // ROWS
HALF = BLOCK // 2
MODEL = 4608
SLAB = MODEL // ROWS
CHUNK = 256
TILE = 128
LISTED = 4 * SHARD + 4 * TILE
DEN_ROWS = 16
PIECE = BLOCK + DEN_ROWS
SEQ = ("z", "xh", "xl")

TO_TANH = SCALE / SOFTCAP
TO_EXP2 = SOFTCAP * math.log2(math.e)

bf16 = jnp.bfloat16
f32 = jnp.float32
VMEM = pl.BlockSpec(memory_space=pltpu.VMEM)
SMEM = pl.BlockSpec(memory_space=pltpu.SMEM)


def local(body, operands, out_shapes, name, scratch=(), flops=0, limit=8 * 2**20):
    return pl.pallas_call(
        body,
        out_shape=out_shapes,
        in_specs=[SMEM] + [VMEM] * (len(operands) - 1),
        out_specs=jax.tree.map(lambda _: VMEM, out_shapes),
        scratch_shapes=list(scratch),
        compiler_params=pltpu.CompilerParams(vmem_limit_bytes=limit),
        cost_estimate=pl.CostEstimate(flops=flops, bytes_accessed=2**20, transcendentals=0),
        name=name,
    )(*operands)


def scalars(ids):
    return ids[0], ids[1], ids[2]


def live_of(ids, shard):
    return ids[3 + shard]


def norm_body(ids, own, received, gain, *refs):
    outs, whole = refs[:ROWS], refs[ROWS]
    _, row, core = scalars(ids)
    kept = own[...].astype(f32)
    other = received[pl.ds(pl.multiple_of(core * HALF, HALF), HALF), :].astype(f32)
    total = jnp.sum(kept * kept, -1, keepdims=True) + jnp.sum(other * other, -1, keepdims=True)
    inverse = lax.rsqrt(total * (1.0 / MODEL) + EPSILON)
    for part in range(2):
        span = slice(part * SLAB, (part + 1) * SLAB)
        for value, slab in ((kept, 2 * core + part), (other, 2 * (1 - core) + part)):
            scale = gain[:, pl.ds(pl.multiple_of(slab * SLAB, HEAD), SLAB)]
            whole[slab] = (value[:, span] * inverse * scale).astype(bf16)
    for step in range(ROWS):
        outs[step][...] = whole[(row + step) & (ROWS - 1)]


def partial_body(steps, split, ids, *refs):
    mine, theirs, weights, outs = refs[:ROWS], refs[ROWS : 2 * ROWS], refs[2 * ROWS], refs[2 * ROWS + 1 :]
    _, row, core = scalars(ids)
    for step, out in zip(steps, outs):
        target = (row + step) & (ROWS - 1)
        if split:
            columns = [
                weights[:, pl.ds(pl.multiple_of((part * ROWS + target) * HEAD, HEAD), HEAD)]
                for part in range(2)
            ]
            columns = jnp.concatenate(columns, 1)
        else:
            columns = weights[:, pl.ds(pl.multiple_of(target * 2 * HEAD, 2 * HEAD), 2 * HEAD)]
        for pieces, side in ((mine, core), (theirs, 1 - core)):
            rows = jnp.concatenate([piece[...] for piece in pieces], 0)
            sums = jnp.dot(rows, columns, preferred_element_type=f32).astype(out.dtype)
            for back in range(ROWS):
                block = (row - back) & (ROWS - 1)
                value = sums[back * HALF : (back + 1) * HALF]
                if len(outs) == len(steps):
                    out[block, side] = value
                else:
                    for half in range(2):
                        outs[half][block, side] = value[:, half * HEAD : (half + 1) * HEAD]


def join_body(ids, up, down, first, second, up_out, down_out):
    up_out[:, :HEAD] = (up[:, :HEAD] + first[...].astype(f32)).astype(bf16)
    up_out[:, HEAD:] = up[:, HEAD:].astype(bf16)
    down_out[:, :HEAD] = down[:, :HEAD].astype(bf16)
    down_out[:, HEAD:] = (down[:, HEAD:] + second[...].astype(f32)).astype(bf16)


def rotate_body(rotated, ids, *refs):
    parts, (cosine, sine, out) = refs[:-3], refs[-3:]
    if len(parts) == 1:
        parts = [parts[0].at[source] for source in range(ROWS)]
    for block in range(ROWS):
        rows = slice(block * BLOCK, (block + 1) * BLOCK)
        total = parts[0][rows].astype(f32)
        for part in parts[1:]:
            total = total + part[rows].astype(f32)
        for half in range(2):
            span = slice(half * HEAD, (half + 1) * HEAD)
            value = total[:, span]
            if half < rotated:
                value = value * cosine[rows] + pltpu.roll(value, HEAD // 2, 1) * sine[rows]
            out[rows, span] = value.astype(bf16)


def key_shards(shard):
    plane, place = shard >> 2, shard & 3
    mirror = PLANE - 1 - place
    chosen = jnp.where(place < 2, plane - 2, plane)
    return (
        shard,
        shard - PLANE,
        (plane - 1) * PLANE + mirror,
        shard - 2 * PLANE,
        chosen * PLANE + mirror,
    )


def mask_values(ids, key_shard, keyval, masked):
    shard = ids[0]
    first = (shard >> 4) << 4
    count = jnp.where(key_shard >= first, live_of(ids, jnp.maximum(key_shard, 0)), 0)
    for start in range(0, SHARD, CHUNK):

        @pl.when(start < count)
        def _():
            alive = (
                lax.broadcasted_iota(jnp.int32, (CHUNK, HEAD), 0) + start < count
            )
            rows = slice(start, start + CHUNK)
            values = keyval[rows, HEAD:].astype(f32)
            masked[rows, :HEAD] = jnp.where(alive, values, 0.0).astype(bf16)
            masked[rows, HEAD:] = jnp.where(alive, 1.0, 0.0).astype(bf16)

    return count


def accumulate(query, query_shard, query_count, blocks, sums, fresh):
    for start in range(0, SHARD, CHUNK):
        tokens = slice(start, start + CHUNK)
        place = start // CHUNK

        @pl.when(start < query_count)
        def _(tokens=tokens, place=place):
            if fresh:
                for head in range(2):
                    sums[head, tokens] = jnp.zeros((CHUNK, 2 * HEAD), f32)
            for key_shard, count, keyval, masked in blocks:
                back = query_shard - key_shard
                chunks = (count + (CHUNK - 1)) // CHUNK
                low = jnp.where(back == 2 * PLANE, place, 0)
                high = jnp.where(back == 0, jnp.minimum(chunks, place + 1), chunks)
                high = jnp.where((back >= 0) & (back <= 2 * PLANE), high, 0)
                edge = (back == 0) | (back == 2 * PLANE)

                def step(chunk, carry, keyval=keyval, masked=masked, back=back, edge=edge):
                    rows = pl.ds(pl.multiple_of(chunk * CHUNK, CHUNK), CHUNK)

                    def work(with_mask):
                        keys = keyval[rows, :HEAD]
                        values = masked[rows, :]
                        if with_mask:
                            key_at = lax.broadcasted_iota(jnp.int32, (CHUNK, CHUNK), 1)
                            query_at = lax.broadcasted_iota(jnp.int32, (CHUNK, CHUNK), 0)
                            ahead = jnp.where(key_at <= query_at, 1, 0)
                            seen = ahead == jnp.where(back == 0, 1, 0)
                        for head in range(2):
                            scores = lax.dot_general(
                                query[tokens, head * HEAD : (head + 1) * HEAD],
                                keys,
                                (((1,), (1,)), ((), ())),
                                preferred_element_type=f32,
                            )
                            weights = jnp.exp2(jnp.tanh(scores * TO_TANH) * TO_EXP2)
                            if with_mask:
                                weights = jnp.where(seen, weights, 0.0)
                            sums[head, tokens] += jnp.dot(
                                weights.astype(bf16), values, preferred_element_type=f32
                            )

                    masked_step = edge & (chunk == place)

                    @pl.when(masked_step)
                    def _():
                        work(True)

                    @pl.when(jnp.logical_not(masked_step))
                    def _():
                        work(False)

                    return carry

                lax.fori_loop(low, high, step, 0)


def early_body(ids, query, own, back1, back2, sums, *masked):
    shard, _, _ = scalars(ids)
    shards = key_shards(shard)
    held = (own, back1, back2)
    shards = (shards[0], shards[1], shards[3])
    blocks = [
        (shards[i], mask_values(ids, shards[i], held[i], masked[i]), held[i], masked[i])
        for i in range(len(held))
    ]
    accumulate(query, shard, live_of(ids, shard), blocks, sums, True)


def late_body(
    ids, query, pair, own, back1, mirror1, back2, chosen, before, out, sums, pair_sums, keys, values
):
    shard, _, _ = scalars(ids)
    side = shard & 1
    partner = shard + 1 - 2 * side
    own_shard, back1_shard, mirror1_shard, back2_shard, chosen_shard = key_shards(shard)
    first = (shard >> 4) << 4
    used = 0
    listed = (
        (own, own_shard, side == 0),
        (back2, back2_shard, side == 1),
        (back1, back1_shard, True),
        (mirror1, mirror1_shard, True),
        (chosen, chosen_shard, True),
    )
    for place, (keyval, key_shard, seen) in enumerate(listed):
        if place == 3:
            common = used
        counted = (key_shard >= first) & seen
        count = jnp.where(counted, live_of(ids, jnp.maximum(key_shard, 0)), 0)
        for start in range(0, SHARD, TILE):

            @pl.when(start < count)
            def _(keyval=keyval, start=start, used=used, count=count):
                alive = lax.broadcasted_iota(jnp.int32, (TILE, HEAD), 0) + start < count
                rows = pl.ds(pl.multiple_of(used * TILE + start, TILE), TILE)
                keys[rows, :] = keyval[start : start + TILE, :HEAD]
                value = keyval[start : start + TILE, HEAD:].astype(f32)
                values[rows, :HEAD] = jnp.where(alive, value, 0.0).astype(bf16)
                values[rows, HEAD:] = jnp.where(alive, 1.0, 0.0).astype(bf16)

        used = used + ((count + (TILE - 1)) >> 7)
    rows = pl.ds(pl.multiple_of(used * TILE, TILE), 3 * TILE)
    keys[rows, :] = jnp.zeros((3 * TILE, HEAD), bf16)
    values[rows, :] = jnp.zeros((3 * TILE, 2 * HEAD), bf16)

    def attend(query, live, low, width, sums):
        for start in range(0, SHARD, CHUNK):
            tokens = slice(start, start + CHUNK)

            @pl.when(start < live)
            def _(tokens=tokens):
                heads = [query[tokens, :HEAD], query[tokens, HEAD:]]
                stacked = jnp.concatenate(heads, 0)
                for head in range(2):
                    sums[head, tokens] = jnp.zeros((CHUNK, 2 * HEAD), f32)

                def step(index, carry):
                    at = pl.ds(pl.multiple_of((low + index * width) * TILE, TILE), width * TILE)
                    scores = lax.dot_general(
                        stacked, keys[at, :], (((1,), (1,)), ((), ())), preferred_element_type=f32
                    )
                    weights = jnp.exp2(jnp.tanh(scores * TO_TANH) * TO_EXP2).astype(bf16)
                    added = jnp.dot(weights, values[at, :], preferred_element_type=f32)
                    for head in range(2):
                        sums[head, tokens] += added[head * CHUNK : (head + 1) * CHUNK]
                    return carry

                lax.fori_loop(0, (used - low + (width - 1)) // width, step, 0)

    count, pair_count = live_of(ids, shard), live_of(ids, partner)
    attend(query, count, common, 4, sums)
    attend(pair, pair_count, 0, 4, pair_sums)
    same = lax.broadcasted_iota(jnp.int32, (BLOCK, HEAD), 0) == lax.broadcasted_iota(
        jnp.int32, (BLOCK, HEAD), 1
    )
    for held, live, owner, earlier in (
        (sums, count, side, before),
        (pair_sums, pair_count, 1 - side, None),
    ):
        for block in range(ROWS):
            start = block * BLOCK

            @pl.when(start < live)
            def _(held=held, owner=owner, earlier=earlier, block=block, start=start):
                target = owner * ROWS + block
                for head in range(2):
                    span = slice(head * HEAD, (head + 1) * HEAD)
                    total = held[head, start : start + BLOCK]
                    if earlier is not None:
                        total = total + earlier[head, start : start + BLOCK]
                    out[target, :BLOCK, span] = total[:, :HEAD].astype(bf16)
                    line = jnp.sum(jnp.where(same, total[:, HEAD:], 0.0), 0, keepdims=True)
                    line = jnp.broadcast_to(line, (8, HEAD))
                    coarse = line.astype(bf16).astype(f32)
                    out[target, BLOCK:, span] = jnp.concatenate([coarse, line - coarse], 0).astype(bf16)


def finish_body(ids, pieces, out):
    shard, row, _ = scalars(ids)
    at = lax.broadcasted_iota(jnp.int32, (BLOCK, HEAD), 0)
    same = at == lax.broadcasted_iota(jnp.int32, (BLOCK, HEAD), 1)
    alive = at + row * BLOCK < live_of(ids, shard)
    for group in range(ROWS):
        for head in range(2):
            span = slice(head * HEAD, (head + 1) * HEAD)
            numer = pieces[group, :BLOCK, span].astype(f32) + pieces[ROWS + group, :BLOCK, span].astype(f32)
            both = pieces[group, BLOCK:, span].astype(f32) + pieces[ROWS + group, BLOCK:, span].astype(f32)
            line = both[0:1] + both[8:9]
            denom = jnp.sum(jnp.where(same, line, 0.0), 1, keepdims=True)
            result = jnp.where(alive, numer * (1.0 / denom), 0.0)
            start = group * 2 * HEAD + head * HEAD
            out[:, start : start + HEAD] = result.astype(bf16)


def along_seq(value, target):
    pairs = []
    for shard in range(32):
        to = target(shard // PLANE, shard % PLANE)
        if to is not None:
            pairs.append((shard, to[0] * PLANE + to[1]))
    return lax.ppermute(value, SEQ, pairs)


def hop(value, places=(0, 1, 2, 3)):
    planes = SEQ_SHARDS // PLANE
    return along_seq(
        value, lambda z, x: (z + 1, x) if x in places and z % planes != planes - 1 else None
    )


def mirrored(value):
    return along_seq(value, lambda z, x: (z, PLANE - 1 - x))


def turned(value):
    planes = SEQ_SHARDS // PLANE

    def target(z, x):
        if x < PLANE // 2:
            return z, PLANE - 1 - x
        return (z + 1, PLANE - 1 - x) if z % planes != planes - 1 else None

    return along_seq(value, target)


def paired(value):
    return along_seq(value, lambda z, x: (z, x ^ 1))


def onward(value, step):
    return lax.ppermute(value, "row", [(row, (row + step) % ROWS) for row in range(ROWS)])


def swapped(value):
    return lax.ppermute(value, "col", [(0, 1), (1, 0)])


def on_device(tokens, norm_gain, w_query, w_keyval, active):
    core = lax.axis_index("col")
    row = lax.axis_index("row")
    shard = lax.axis_index(SEQ)
    ids = jnp.concatenate([jnp.stack([shard, row, core]).astype(jnp.int32), active])
    sds = jax.ShapeDtypeStruct

    received = swapped(tokens)
    kept = lax.dynamic_slice_in_dim(tokens, core * HALF, HALF, 0)
    gain = norm_gain.reshape(1, MODEL)
    piece = sds((HALF, SLAB), bf16)
    normed = local(
        norm_body,
        (ids, kept, received, gain),
        [piece] * ROWS,
        "norm",
        scratch=[pltpu.VMEM((ROWS, HALF, SLAB), bf16)],
    )
    far_piece = onward(normed[2], 2)
    mine = [normed[0], onward(normed[1], 1), far_piece, onward(normed[3], 3)]
    theirs = [swapped(value) for value in mine]
    mine, place = lax.optimization_barrier((mine, shard))

    half = HEAD // 2
    positions = (place % SEQ_SHARDS) * SHARD + jnp.arange(SHARD, dtype=jnp.int32)
    freqs = 10000.0 ** (-2.0 * jnp.arange(half, dtype=f32) / HEAD)
    angles = positions.astype(f32)[:, None] * freqs[None, :]
    cosine, sine = jnp.cos(angles), jnp.sin(angles)
    cosine = jnp.concatenate([cosine, cosine], 1)
    sine = jnp.concatenate([-sine, sine], 1)

    flat = w_keyval.reshape(SLAB, 2 * ROWS * HEAD)
    held = sds((SHARD, 2 * HEAD), bf16)
    split = (ROWS, 2, HALF, 2 * HEAD)
    flops = 2 * SHARD * SLAB * 8 * HEAD

    def sums_across(mine, theirs, weights, split_columns, steps, kind, name, count=1):
        parts = local(
            functools.partial(partial_body, steps, split_columns),
            (ids, *mine, *theirs, weights),
            [sds(split[:3] + (2 * HEAD // count,), kind)] * (len(steps) * count),
            name,
            flops=flops * len(steps) // ROWS,
        )
        return [value.reshape(SHARD, 2 * HEAD // count) for value in parts]

    def joined(up, down, first, second, name):
        return local(join_body, (ids, up, down, first, second), [held, held], name)

    first, second = sums_across(mine, theirs, flat, True, (2,), bf16, "keyval_far", 2)
    mine, theirs, first, second = lax.optimization_barrier((mine, theirs, first, second))
    first, second = onward(first, 1), onward(second, 3)
    up, down, kept = sums_across(mine, theirs, flat, True, (1, 3, 0), f32, "keyval_near")
    mine, theirs, kept, cosine, sine = lax.optimization_barrier((mine, theirs, kept, cosine, sine))
    up, down = joined(up, down, first, second, "keyval_join")
    mine, theirs, up, down = lax.optimization_barrier((mine, theirs, up, down))
    up, down = onward(up, 1), onward(down, 3)
    steps = (2, 1, 3, 0)
    query_sums = sums_across(mine, theirs, w_query, False, steps, bf16, "query_partial")
    own = local(
        functools.partial(rotate_body, 1), (ids, kept, up, down, cosine, sine), held, "keyval_rotate"
    )
    query_sums, own = lax.optimization_barrier((query_sums, own))
    query_sums = [onward(value, step) if step else value for value, step in zip(query_sums, steps)]

    back1 = hop(own)
    back2 = hop(back1)
    across = turned(back1)
    opposite = mirrored(own)
    lower = lax.axis_index("xh") == 0
    raised = hop(opposite, (0, 1))
    mirror1 = jnp.where(lower, raised, across)
    chosen = jnp.where(lower, across, opposite)

    query_sums, back2 = lax.optimization_barrier((query_sums, back2))
    query = local(
        functools.partial(rotate_body, 2), (ids, *query_sums, cosine, sine), held, "query_rotate"
    )
    pair = paired(query)

    sums_shape = (2, SHARD, 2 * HEAD)
    masked = pltpu.VMEM((SHARD, 2 * HEAD), bf16)
    before = local(
        early_body,
        (ids, query, own, back1, back2),
        sds(sums_shape, f32),
        "attend_early",
        scratch=[masked] * 3,
        flops=2**31,
    )
    pieces = local(
        late_body,
        (ids, query, pair, own, back1, mirror1, back2, chosen, before),
        sds((2 * ROWS, PIECE, 2 * HEAD), bf16),
        "attend_late",
        scratch=[
            pltpu.VMEM(sums_shape, f32),
            pltpu.VMEM(sums_shape, f32),
            pltpu.VMEM((LISTED, HEAD), bf16),
            pltpu.VMEM((LISTED, 2 * HEAD), bf16),
        ],
        flops=2**31,
        limit=16 * 2**20,
    )
    returned = lax.all_to_all(pieces, ("xl", "row"), 0, 0)
    return local(finish_body, (ids, returned), sds((BLOCK, ROWS * 2 * HEAD), bf16), "finish")


def solution(mesh):
    fine = Mesh(mesh.devices.reshape(8, 2, 2, ROWS, 2), SEQ + ("row", "col"))
    tokens_spec = P(SEQ + ("row",), "col")
    placed = (tokens_spec, P(), P("row", "col"), P("row", None, "col"), P())
    return jax.shard_map(
        on_device, mesh=fine, in_specs=placed, out_specs=tokens_spec, check_vma=False
    )
```

```python
import functools
import math

import jax
import jax.numpy as jnp
from jax import lax
from jax.experimental import pallas as pl
from jax.experimental.pallas import tpu as pltpu
from jax.sharding import Mesh, PartitionSpec as P

SCALE = 1.0 / 12.0
SOFTCAP = 50.0
EPSILON = 1e-06

HEAD = 128
SHARD = 512
SEQ_SHARDS = 16
PLANE = 4
ROWS = 4
BLOCK = SHARD // ROWS
HALF = BLOCK // 2
MODEL = 4608
SLAB = MODEL // ROWS
CHUNK = 256
TILE = 128
LISTED = 4 * SHARD + 4 * TILE
DEN_ROWS = 16
PIECE = BLOCK + DEN_ROWS
SEQ = ("z", "xh", "xl")

TO_TANH = SCALE / SOFTCAP
TO_EXP2 = SOFTCAP * math.log2(math.e)

bf16 = jnp.bfloat16
f32 = jnp.float32
VMEM = pl.BlockSpec(memory_space=pltpu.VMEM)
SMEM = pl.BlockSpec(memory_space=pltpu.SMEM)


def local(body, operands, out_shapes, name, scratch=(), flops=0, limit=8 * 2**20):
    return pl.pallas_call(
        body,
        out_shape=out_shapes,
        in_specs=[SMEM] + [VMEM] * (len(operands) - 1),
        out_specs=jax.tree.map(lambda _: VMEM, out_shapes),
        scratch_shapes=list(scratch),
        compiler_params=pltpu.CompilerParams(vmem_limit_bytes=limit),
        cost_estimate=pl.CostEstimate(flops=flops, bytes_accessed=2**20, transcendentals=0),
        name=name,
    )(*operands)


def scalars(ids):
    return ids[0], ids[1], ids[2]


def live_of(ids, shard):
    return ids[3 + shard]


def norm_body(ids, own, received, gain, *refs):
    outs, whole = refs[:ROWS], refs[ROWS]
    _, row, core = scalars(ids)
    kept = own[...].astype(f32)
    other = received[pl.ds(pl.multiple_of(core * HALF, HALF), HALF), :].astype(f32)
    total = jnp.sum(kept * kept, -1, keepdims=True) + jnp.sum(other * other, -1, keepdims=True)
    inverse = lax.rsqrt(total * (1.0 / MODEL) + EPSILON)
    for part in range(2):
        span = slice(part * SLAB, (part + 1) * SLAB)
        for value, slab in ((kept, 2 * core + part), (other, 2 * (1 - core) + part)):
            scale = gain[:, pl.ds(pl.multiple_of(slab * SLAB, HEAD), SLAB)]
            whole[slab] = (value[:, span] * inverse * scale).astype(bf16)
    for step in range(ROWS):
        outs[step][...] = whole[(row + step) & (ROWS - 1)]


def partial_body(steps, split, ids, *refs):
    mine, theirs, weights, outs = refs[:ROWS], refs[ROWS : 2 * ROWS], refs[2 * ROWS], refs[2 * ROWS + 1 :]
    _, row, core = scalars(ids)
    for step, out in zip(steps, outs):
        target = (row + step) & (ROWS - 1)
        if split:
            columns = [
                weights[:, pl.ds(pl.multiple_of((part * ROWS + target) * HEAD, HEAD), HEAD)]
                for part in range(2)
            ]
            columns = jnp.concatenate(columns, 1)
        else:
            columns = weights[:, pl.ds(pl.multiple_of(target * 2 * HEAD, 2 * HEAD), 2 * HEAD)]
        for pieces, side in ((mine, core), (theirs, 1 - core)):
            rows = jnp.concatenate([piece[...] for piece in pieces], 0)
            sums = jnp.dot(rows, columns, preferred_element_type=f32).astype(out.dtype)
            for back in range(ROWS):
                block = (row - back) & (ROWS - 1)
                value = sums[back * HALF : (back + 1) * HALF]
                if len(outs) == len(steps):
                    out[block, side] = value
                else:
                    for half in range(2):
                        outs[half][block, side] = value[:, half * HEAD : (half + 1) * HEAD]


def join_body(ids, up, down, first, second, up_out, down_out):
    up_out[:, :HEAD] = (up[:, :HEAD] + first[...].astype(f32)).astype(bf16)
    up_out[:, HEAD:] = up[:, HEAD:].astype(bf16)
    down_out[:, :HEAD] = down[:, :HEAD].astype(bf16)
    down_out[:, HEAD:] = (down[:, HEAD:] + second[...].astype(f32)).astype(bf16)


def rotate_body(rotated, ids, *refs):
    parts, (cosine, sine, out) = refs[:-3], refs[-3:]
    if len(parts) == 1:
        parts = [parts[0].at[source] for source in range(ROWS)]
    for block in range(ROWS):
        rows = slice(block * BLOCK, (block + 1) * BLOCK)
        total = parts[0][rows].astype(f32)
        for part in parts[1:]:
            total = total + part[rows].astype(f32)
        for half in range(2):
            span = slice(half * HEAD, (half + 1) * HEAD)
            value = total[:, span]
            if half < rotated:
                value = value * cosine[rows] + pltpu.roll(value, HEAD // 2, 1) * sine[rows]
            out[rows, span] = value.astype(bf16)


def key_shards(shard):
    plane, place = shard >> 2, shard & 3
    mirror = PLANE - 1 - place
    chosen = jnp.where(place < 2, plane - 2, plane)
    return (
        shard,
        shard - PLANE,
        (plane - 1) * PLANE + mirror,
        shard - 2 * PLANE,
        chosen * PLANE + mirror,
    )


def mask_values(ids, key_shard, keyval, masked):
    shard = ids[0]
    first = (shard >> 4) << 4
    count = jnp.where(key_shard >= first, live_of(ids, jnp.maximum(key_shard, 0)), 0)
    for start in range(0, SHARD, CHUNK):

        @pl.when(start < count)
        def _():
            alive = (
                lax.broadcasted_iota(jnp.int32, (CHUNK, HEAD), 0) + start < count
            )
            rows = slice(start, start + CHUNK)
            values = keyval[rows, HEAD:].astype(f32)
            masked[rows, :HEAD] = jnp.where(alive, values, 0.0).astype(bf16)
            masked[rows, HEAD:] = jnp.where(alive, 1.0, 0.0).astype(bf16)

    return count


def accumulate(query, query_shard, query_count, blocks, sums, fresh):
    for start in range(0, SHARD, CHUNK):
        tokens = slice(start, start + CHUNK)
        place = start // CHUNK

        @pl.when(start < query_count)
        def _(tokens=tokens, place=place):
            if fresh:
                for head in range(2):
                    sums[head, tokens] = jnp.zeros((CHUNK, 2 * HEAD), f32)
            for key_shard, count, keyval, masked in blocks:
                back = query_shard - key_shard
                chunks = (count + (CHUNK - 1)) // CHUNK
                low = jnp.where(back == 2 * PLANE, place, 0)
                high = jnp.where(back == 0, jnp.minimum(chunks, place + 1), chunks)
                high = jnp.where((back >= 0) & (back <= 2 * PLANE), high, 0)
                edge = (back == 0) | (back == 2 * PLANE)

                def step(chunk, carry, keyval=keyval, masked=masked, back=back, edge=edge):
                    rows = pl.ds(pl.multiple_of(chunk * CHUNK, CHUNK), CHUNK)

                    def work(with_mask):
                        keys = keyval[rows, :HEAD]
                        values = masked[rows, :]
                        if with_mask:
                            key_at = lax.broadcasted_iota(jnp.int32, (CHUNK, CHUNK), 1)
                            query_at = lax.broadcasted_iota(jnp.int32, (CHUNK, CHUNK), 0)
                            ahead = jnp.where(key_at <= query_at, 1, 0)
                            seen = ahead == jnp.where(back == 0, 1, 0)
                        for head in range(2):
                            scores = lax.dot_general(
                                query[tokens, head * HEAD : (head + 1) * HEAD],
                                keys,
                                (((1,), (1,)), ((), ())),
                                preferred_element_type=f32,
                            )
                            weights = jnp.exp2(jnp.tanh(scores * TO_TANH) * TO_EXP2)
                            if with_mask:
                                weights = jnp.where(seen, weights, 0.0)
                            sums[head, tokens] += jnp.dot(
                                weights.astype(bf16), values, preferred_element_type=f32
                            )

                    masked_step = edge & (chunk == place)

                    @pl.when(masked_step)
                    def _():
                        work(True)

                    @pl.when(jnp.logical_not(masked_step))
                    def _():
                        work(False)

                    return carry

                lax.fori_loop(low, high, step, 0)


def early_body(ids, query, own, back1, back2, sums, *masked):
    shard, _, _ = scalars(ids)
    shards = key_shards(shard)
    held = (own, back1, back2)
    shards = (shards[0], shards[1], shards[3])
    blocks = [
        (shards[i], mask_values(ids, shards[i], held[i], masked[i]), held[i], masked[i])
        for i in range(len(held))
    ]
    accumulate(query, shard, live_of(ids, shard), blocks, sums, True)


def late_body(
    ids, query, pair, own, back1, back2, raised, opposite, across, before, out, sums, pair_sums, keys, values
):
    shard, _, _ = scalars(ids)
    side = shard & 1
    partner = shard + 1 - 2 * side
    own_shard, back1_shard, mirror1_shard, back2_shard, chosen_shard = key_shards(shard)
    first = (shard >> 4) << 4
    lower = (shard & 2) == 0
    used = 0
    listed = (
        (own, own_shard, side == 0),
        (back2, back2_shard, side == 1),
        (back1, back1_shard, True),
        (raised, mirror1_shard, lower),
        (opposite, chosen_shard, jnp.logical_not(lower)),
        (across, jnp.where(lower, chosen_shard, mirror1_shard), True),
    )
    for place, (keyval, key_shard, seen) in enumerate(listed):
        if place == 3:
            common = used
        counted = (key_shard >= first) & seen
        count = jnp.where(counted, live_of(ids, jnp.maximum(key_shard, 0)), 0)
        for start in range(0, SHARD, TILE):

            @pl.when(start < count)
            def _(keyval=keyval, start=start, used=used, count=count):
                alive = lax.broadcasted_iota(jnp.int32, (TILE, HEAD), 0) + start < count
                rows = pl.ds(pl.multiple_of(used * TILE + start, TILE), TILE)
                keys[rows, :] = keyval[start : start + TILE, :HEAD]
                value = keyval[start : start + TILE, HEAD:].astype(f32)
                values[rows, :HEAD] = jnp.where(alive, value, 0.0).astype(bf16)
                values[rows, HEAD:] = jnp.where(alive, 1.0, 0.0).astype(bf16)

        used = used + ((count + (TILE - 1)) >> 7)
    rows = pl.ds(pl.multiple_of(used * TILE, TILE), 3 * TILE)
    keys[rows, :] = jnp.zeros((3 * TILE, HEAD), bf16)
    values[rows, :] = jnp.zeros((3 * TILE, 2 * HEAD), bf16)

    def attend(query, live, low, width, sums):
        for start in range(0, SHARD, CHUNK):
            tokens = slice(start, start + CHUNK)

            @pl.when(start < live)
            def _(tokens=tokens):
                heads = [query[tokens, :HEAD], query[tokens, HEAD:]]
                stacked = jnp.concatenate(heads, 0)
                for head in range(2):
                    sums[head, tokens] = jnp.zeros((CHUNK, 2 * HEAD), f32)

                def step(index, carry):
                    at = pl.ds(pl.multiple_of((low + index * width) * TILE, TILE), width * TILE)
                    scores = lax.dot_general(
                        stacked, keys[at, :], (((1,), (1,)), ((), ())), preferred_element_type=f32
                    )
                    weights = jnp.exp2(jnp.tanh(scores * TO_TANH) * TO_EXP2).astype(bf16)
                    added = jnp.dot(weights, values[at, :], preferred_element_type=f32)
                    for head in range(2):
                        sums[head, tokens] += added[head * CHUNK : (head + 1) * CHUNK]
                    return carry

                lax.fori_loop(0, (used - low + (width - 1)) // width, step, 0)

    count, pair_count = live_of(ids, shard), live_of(ids, partner)
    attend(query, count, common, 4, sums)
    attend(pair, pair_count, 0, 4, pair_sums)
    same = lax.broadcasted_iota(jnp.int32, (BLOCK, HEAD), 0) == lax.broadcasted_iota(
        jnp.int32, (BLOCK, HEAD), 1
    )
    for held, live, owner, earlier in (
        (sums, count, side, before),
        (pair_sums, pair_count, 1 - side, None),
    ):
        for block in range(ROWS):
            start = block * BLOCK

            @pl.when(start < live)
            def _(held=held, owner=owner, earlier=earlier, block=block, start=start):
                target = owner * ROWS + block
                for head in range(2):
                    span = slice(head * HEAD, (head + 1) * HEAD)
                    total = held[head, start : start + BLOCK]
                    if earlier is not None:
                        total = total + earlier[head, start : start + BLOCK]
                    out[target, :BLOCK, span] = total[:, :HEAD].astype(bf16)
                    line = jnp.sum(jnp.where(same, total[:, HEAD:], 0.0), 0, keepdims=True)
                    line = jnp.broadcast_to(line, (8, HEAD))
                    coarse = line.astype(bf16).astype(f32)
                    out[target, BLOCK:, span] = jnp.concatenate([coarse, line - coarse], 0).astype(bf16)


def finish_body(ids, pieces, out):
    shard, row, _ = scalars(ids)
    at = lax.broadcasted_iota(jnp.int32, (BLOCK, HEAD), 0)
    same = at == lax.broadcasted_iota(jnp.int32, (BLOCK, HEAD), 1)
    alive = at + row * BLOCK < live_of(ids, shard)
    for group in range(ROWS):
        for head in range(2):
            span = slice(head * HEAD, (head + 1) * HEAD)
            numer = pieces[group, :BLOCK, span].astype(f32) + pieces[ROWS + group, :BLOCK, span].astype(f32)
            both = pieces[group, BLOCK:, span].astype(f32) + pieces[ROWS + group, BLOCK:, span].astype(f32)
            line = both[0:1] + both[8:9]
            denom = jnp.sum(jnp.where(same, line, 0.0), 1, keepdims=True)
            result = jnp.where(alive, numer * (1.0 / denom), 0.0)
            start = group * 2 * HEAD + head * HEAD
            out[:, start : start + HEAD] = result.astype(bf16)


def along_seq(value, target):
    pairs = []
    for shard in range(32):
        to = target(shard // PLANE, shard % PLANE)
        if to is not None:
            pairs.append((shard, to[0] * PLANE + to[1]))
    return lax.ppermute(value, SEQ, pairs)


def hop(value, places=(0, 1, 2, 3)):
    planes = SEQ_SHARDS // PLANE
    return along_seq(
        value, lambda z, x: (z + 1, x) if x in places and z % planes != planes - 1 else None
    )


def mirrored(value):
    return along_seq(value, lambda z, x: (z, PLANE - 1 - x))


def turned(value):
    planes = SEQ_SHARDS // PLANE

    def target(z, x):
        if x < PLANE // 2:
            return z, PLANE - 1 - x
        return (z + 1, PLANE - 1 - x) if z % planes != planes - 1 else None

    return along_seq(value, target)


def paired(value):
    return along_seq(value, lambda z, x: (z, x ^ 1))


def onward(value, step):
    return lax.ppermute(value, "row", [(row, (row + step) % ROWS) for row in range(ROWS)])


def swapped(value):
    return lax.ppermute(value, "col", [(0, 1), (1, 0)])


def on_device(tokens, norm_gain, w_query, w_keyval, active):
    core = lax.axis_index("col")
    row = lax.axis_index("row")
    shard = lax.axis_index(SEQ)
    ids = jnp.concatenate([jnp.stack([shard, row, core]).astype(jnp.int32), active])
    sds = jax.ShapeDtypeStruct

    received = swapped(tokens)
    kept = lax.dynamic_slice_in_dim(tokens, core * HALF, HALF, 0)
    gain = norm_gain.reshape(1, MODEL)
    piece = sds((HALF, SLAB), bf16)
    normed = local(
        norm_body,
        (ids, kept, received, gain),
        [piece] * ROWS,
        "norm",
        scratch=[pltpu.VMEM((ROWS, HALF, SLAB), bf16)],
    )
    far_piece = onward(normed[2], 2)
    mine = [normed[0], onward(normed[1], 1), far_piece, onward(normed[3], 3)]
    theirs = [swapped(value) for value in mine]
    mine, place = lax.optimization_barrier((mine, shard))

    half = HEAD // 2
    positions = (place % SEQ_SHARDS) * SHARD + jnp.arange(SHARD, dtype=jnp.int32)
    freqs = 10000.0 ** (-2.0 * jnp.arange(half, dtype=f32) / HEAD)
    angles = positions.astype(f32)[:, None] * freqs[None, :]
    cosine, sine = jnp.cos(angles), jnp.sin(angles)
    cosine = jnp.concatenate([cosine, cosine], 1)
    sine = jnp.concatenate([-sine, sine], 1)

    flat = w_keyval.reshape(SLAB, 2 * ROWS * HEAD)
    held = sds((SHARD, 2 * HEAD), bf16)
    split = (ROWS, 2, HALF, 2 * HEAD)
    flops = 2 * SHARD * SLAB * 8 * HEAD

    def sums_across(mine, theirs, weights, split_columns, steps, kind, name, count=1):
        parts = local(
            functools.partial(partial_body, steps, split_columns),
            (ids, *mine, *theirs, weights),
            [sds(split[:3] + (2 * HEAD // count,), kind)] * (len(steps) * count),
            name,
            flops=flops * len(steps) // ROWS,
        )
        return [value.reshape(SHARD, 2 * HEAD // count) for value in parts]

    def joined(up, down, first, second, name):
        return local(join_body, (ids, up, down, first, second), [held, held], name)

    first, second = sums_across(mine, theirs, flat, True, (2,), bf16, "keyval_far", 2)
    mine, theirs, first, second = lax.optimization_barrier((mine, theirs, first, second))
    first, second = onward(first, 1), onward(second, 3)
    up, down, kept = sums_across(mine, theirs, flat, True, (1, 3, 0), f32, "keyval_near")
    mine, theirs, kept, cosine, sine = lax.optimization_barrier((mine, theirs, kept, cosine, sine))
    up, down = joined(up, down, first, second, "keyval_join")
    mine, theirs, up, down = lax.optimization_barrier((mine, theirs, up, down))
    up, down = onward(up, 1), onward(down, 3)
    steps = (2, 1, 3, 0)
    query_sums = sums_across(mine, theirs, w_query, False, steps, bf16, "query_partial")
    own = local(
        functools.partial(rotate_body, 1), (ids, kept, up, down, cosine, sine), held, "keyval_rotate"
    )
    query_sums, own = lax.optimization_barrier((query_sums, own))
    query_sums = [onward(value, step) if step else value for value, step in zip(query_sums, steps)]

    back1 = hop(own)
    back2 = hop(back1)
    across = turned(back1)
    opposite = mirrored(own)
    raised = hop(opposite, (0, 1))

    query_sums, back2 = lax.optimization_barrier((query_sums, back2))
    query = local(
        functools.partial(rotate_body, 2), (ids, *query_sums, cosine, sine), held, "query_rotate"
    )
    pair = paired(query)

    sums_shape = (2, SHARD, 2 * HEAD)
    masked = pltpu.VMEM((SHARD, 2 * HEAD), bf16)
    before = local(
        early_body,
        (ids, query, own, back1, back2),
        sds(sums_shape, f32),
        "attend_early",
        scratch=[masked] * 3,
        flops=2**31,
    )
    pieces = local(
        late_body,
        (ids, query, pair, own, back1, back2, raised, opposite, across, before),
        sds((2 * ROWS, PIECE, 2 * HEAD), bf16),
        "attend_late",
        scratch=[
            pltpu.VMEM(sums_shape, f32),
            pltpu.VMEM(sums_shape, f32),
            pltpu.VMEM((LISTED, HEAD), bf16),
            pltpu.VMEM((LISTED, 2 * HEAD), bf16),
        ],
        flops=2**31,
        limit=16 * 2**20,
    )
    returned = lax.all_to_all(pieces, ("xl", "row"), 0, 0)
    return local(finish_body, (ids, returned), sds((BLOCK, ROWS * 2 * HEAD), bf16), "finish")


def solution(mesh):
    fine = Mesh(mesh.devices.reshape(8, 2, 2, ROWS, 2), SEQ + ("row", "col"))
    tokens_spec = P(SEQ + ("row",), "col")
    placed = (tokens_spec, P(), P("row", "col"), P("row", None, "col"), P())
    return jax.shard_map(
        on_device, mesh=fine, in_specs=placed, out_specs=tokens_spec, check_vma=False
    )
```
